128 devices in a mesh: dp: 2 (over x_lo), ctx: 8 (over z, core), expert: 8 (over y, x_hi).
Axes of the slice: x: 4 (x_hi: 2, x_lo: 2; x = x_hi * 2 + x_lo), y: 4, z: 4, core: 2. Of those that a mesh axis runs over, the one named last changes fastest.
Arguments:
- tokens: bfloat16 [16, 1024, 1024], P(('dp', 'expert'), 'ctx'), may hold values from -6 to 6
- doc_ids: int32 [16, 1024], P(('dp', 'expert')), may hold values from 0 to 2, as said below
- gain_attn: bfloat16 [1024], replicated, may hold values from 0.25 to 1.75
- w_qkv: bfloat16 [1024, 2048], replicated, may hold values from -0.25 to 0.25
- w_out: bfloat16 [1024, 1024], replicated, may hold values from -0.75 to 0.75
- gain_ffn: bfloat16 [1024], replicated, may hold values from 0.25 to 1.75
- w_router: bfloat16 [1024, 32], replicated, may hold values from -0.09375 to 0.09375
- routes: int32 [16, 1024, 8], P(('dp', 'expert'), 'ctx'), may hold values from 0 to 31, all different within a row; in each aligned block of 128 rows (0 to 127, 128 to 255, ..., all dimensions but the last counted through in order) at most 64 rows name the same one
- w_gate: bfloat16 [32, 1024, 512], P('expert'), may hold values from -0.1875 to 0.1875
- w_up: bfloat16 [32, 1024, 512], P('expert'), may hold values from -0.1875 to 0.1875
- w_down: bfloat16 [32, 512, 1024], P('expert'), may hold values from -1 to 1
- grad_output: bfloat16 [16, 1024, 1024], P(('dp', 'expert'), 'ctx'), may hold values from -6 to 6
Outputs:
- output: bfloat16 [16, 1024, 1024], P(('dp', 'expert'), 'ctx')
- grad_tokens: bfloat16 [16, 1024, 1024], P(('dp', 'expert'), 'ctx')
- grad_gain_attn: float32 [1024], P(('dp', 'ctx', 'expert'))
- grad_w_qkv: float32 [1024, 2048], P(('dp', 'ctx', 'expert'))
- grad_w_out: float32 [1024, 1024], P(('dp', 'ctx', 'expert'))
- grad_gain_ffn: float32 [1024], P(('dp', 'ctx', 'expert'))
- grad_w_router: float32 [1024, 32], P(('dp', 'ctx', 'expert'))
- grad_w_gate: float32 [32, 1024, 512], P('expert', ('dp', 'ctx'))
- grad_w_up: float32 [32, 1024, 512], P('expert', ('dp', 'ctx'))
- grad_w_down: float32 [32, 512, 1024], P('expert', ('dp', 'ctx'))
The draws below stay inside these ranges and needn't reach their ends.
Inputs may be any that keep to these rules, and one draw needn't show every extreme that they name: `doc_ids`: in each sequence the numbers are 0, then 1, then 2, never falling; document 1 begins within the first 128 positions and ends within the last 128. `routes`: A token names 8 different experts. Within each aligned block of 128 tokens (the tokens of one device) no expert is named by more than 64 tokens, a bound that some block reaches.
All inputs are finite; a program needn't handle non-finite values.
Results may differ from the reference program's by a relative error of at most 0.028.
Values may be sent and summed in bfloat16 or wider, within the bound.
No kernel may reach another device: no remote copies, remote signals or barrier semaphores. Data moves between devices by JAX's collectives and lax.ppermute only.
A program may use at most 192 MiB of HBM per device.

```python
import math
import jax
import jax.numpy as jnp
import numpy as np
from jax import lax

D = 1024
FF = 512
QH = 16
KVH = 8
HD = 64
TOP = 8
EXPERTS = 32
LENGTH = 1024
TOK_DEV = 128
SEQS = 16
CAP = 64
QKV = 2048
ATT = 1024


def draw_doc_ids(key, part):
    key = jax.random.fold_in(key, 11)
    first_key, second_key = jax.random.split(key)
    first_cut = jax.random.randint(first_key, (SEQS, 1), 1, TOK_DEV)
    second_cut = jax.random.randint(second_key, (SEQS, 1), LENGTH - TOK_DEV + 1, LENGTH)
    places = jnp.arange(LENGTH, dtype=jnp.int32)[None, :]
    return (places >= first_cut).astype(jnp.int32) + (places >= second_cut).astype(jnp.int32)


def levels(key, extent, pieces, smallest, high):
    gain = 1.0
    for dim, blocks in pieces:
        steps = jax.random.uniform(jax.random.fold_in(jax.random.fold_in(key, 6), dim), (blocks,), jnp.float32, smallest / len(pieces), high / len(pieces))
        gain = gain * jnp.repeat(jnp.exp(steps), extent[dim] // blocks).reshape((-1,) + (1,) * (len(extent) - 1 - dim))
    return gain


def deal_out(key, own, number, rows, count, top, most, skew):
    order = jax.random.permutation(key, count)
    packed, usual = load_shares(count, rows * top, most, skew, True), load_shares(count, rows * top, most, skew, False)
    places = jnp.arange(count)

    def named(lengths, turn):
        used = int((lengths > 0).sum())
        fixed = max(1, used // 4)
        passed = fixed + (places - fixed + turn * (used - fixed)) % max(1, count - fixed)
        return jnp.zeros((count,), jnp.int32).at[order[jnp.where(places < fixed, places, passed)]].set(jnp.asarray(lengths, jnp.int32))

    lengths = jnp.where(number % 4 == 0, named(packed, number // 4), named(usual, number - number // 4 - 1))
    mixed = jax.random.permutation(jax.random.fold_in(own, 3), count)
    donor, taker = mixed[0:count // 2 * 2:2], mixed[1:count // 2 * 2:2]
    margin = jnp.minimum(lengths[donor] - 1, most - lengths[taker]) // 2
    margin = jnp.where((donor == order[0]) | (taker == order[0]) | (lengths[taker] == 0), 0, jnp.maximum(margin, 0))
    passed = jax.random.randint(jax.random.fold_in(own, 4), (count // 2,), 0, 1 << 20) % (margin + 1)
    lengths = lengths.at[donor].add(-passed).at[taker].add(passed)
    members = jnp.searchsorted(jnp.cumsum(lengths), jnp.arange(rows * top), side="right").astype(jnp.int32)
    table = members.reshape(top, rows).T
    table = table[jax.random.permutation(jax.random.fold_in(own, 1), rows)]
    turn = jax.random.randint(jax.random.fold_in(own, 2), (rows, 1), 0, top)
    return jnp.take_along_axis(table, (jnp.arange(top)[None, :] + turn) % top, axis=1)


def load_shares(amount, total, bound, slope, full):
    weights = [(1 << 20) // math.isqrt(grade ** slope) + 1 for grade in range(1, amount + 1)]
    largest = bound if full else min(bound, max(-(-total // amount), total * weights[0] // sum(weights)))
    least = 1 if total - largest >= amount - 1 else 0
    given, rest = [largest] + [least] * (amount - 1), total - largest - least * (amount - 1)
    while rest > 0:
        free = [i for i in range(1, amount) if given[i] < largest] or [i for i in range(1, amount) if given[i] < bound]
        mass, remaining = sum([weights[i] for i in free]), rest
        for i in free:
            addition = min(bound - given[i], max(1, remaining * weights[i] // mass), rest)
            given[i] = given[i] + addition
            rest = rest - addition
    return np.array(given)


def gaussian(stream_key, shape, width, bound, cuts=(), kind=jnp.bfloat16):
    gain = levels(stream_key, shape, cuts, -0.22, 0.18) if cuts else 1.0
    values = jax.random.normal(stream_key, shape, jnp.float32) * width * gain
    return jnp.minimum(jnp.maximum(values, -bound), bound).astype(kind)


def setup_inputs(seed: int = 0) -> dict:
    streams_of = jax.random.split(jax.random.key(seed), 13)
    tokens = gaussian(streams_of[0], (SEQS, LENGTH, D), 1.0, 6.0, ((0, 16), (1, 8)))
    doc_ids = draw_doc_ids(jax.random.fold_in(streams_of[12], 71), 0)
    gain_attn = jnp.clip(1.0 + 0.15 * jax.random.normal(streams_of[2], (D,), jnp.float32), 0.25, 1.75).astype(jnp.bfloat16)
    w_qkv = gaussian(streams_of[3], (D, QKV), (D // 2) ** -0.5, 0.25)
    w_out = gaussian(streams_of[4], (ATT, D), (D // 16) ** -0.5, 0.75)
    gain_ffn = jnp.clip(1.0 + 0.15 * jax.random.normal(streams_of[5], (D,), jnp.float32), 0.25, 1.75).astype(jnp.bfloat16)
    w_router = gaussian(streams_of[6], (D, EXPERTS), (4 * D) ** -0.5, 0.09375)
    routes_keys = jax.random.split(jax.random.fold_in(streams_of[7], 1), SEQS * LENGTH // TOK_DEV)
    routes_turns = jax.random.permutation(jax.random.fold_in(streams_of[7], 3), SEQS * LENGTH // TOK_DEV)
    routes = jax.vmap(lambda own, number: deal_out(jax.random.fold_in(streams_of[7], 2), own, number, TOK_DEV, EXPERTS, TOP, CAP, 2))(routes_keys, routes_turns).reshape((SEQS, LENGTH, TOP))
    w_gate = gaussian(streams_of[8], (EXPERTS, D, FF), D ** -0.5, 0.1875, ((0, 8),))
    w_up = gaussian(streams_of[9], (EXPERTS, D, FF), D ** -0.5, 0.1875, ((0, 8),))
    w_down = gaussian(streams_of[10], (EXPERTS, FF, D), (FF // 16) ** -0.5, 1.0, ((0, 8),))
    grad_output = gaussian(streams_of[11], (SEQS, LENGTH, D), 1.0, 6.0, ((0, 16), (1, 8)))
    return dict(tokens=tokens, doc_ids=doc_ids, gain_attn=gain_attn, w_qkv=w_qkv, w_out=w_out, gain_ffn=gain_ffn, w_router=w_router, routes=routes, w_gate=w_gate, w_up=w_up, w_down=w_down, grad_output=grad_output)


@jax.custom_vjp
def low(v):
    return lax.optimization_barrier(v.astype(jnp.bfloat16)).astype(jnp.float32)

@jax.custom_vjp
def low_back(v):
    return v

def low_keep(v):
    return (low(v), None)

def low_pass(kept, grad):
    return (grad,)

def back_keep(v):
    return (v, None)

def back_low(kept, grad):
    return (low(grad),)
low.defvjp(low_keep, low_pass)
low_back.defvjp(back_keep, back_low)
precise = lax.Precision.HIGHEST

def rms_scale(values, gain_vec):
    mean_square = lax.optimization_barrier(jnp.mean(values * values, axis=-1, keepdims=True))
    return values * lax.rsqrt(mean_square + 1e-06) * gain_vec

def rotate(values, places, factor):
    half_dim = values.shape[-1] // 2
    frequency = 10000.0 ** (-jnp.arange(half_dim).astype(jnp.float32) / half_dim)
    angles = places.astype(jnp.float32)[:, None] * frequency[None, :]
    cosine = jnp.cos(angles)[:, None, :]
    sine_part = factor * jnp.sin(angles)[:, None, :]
    first_half = values[..., :half_dim]
    second = values[..., half_dim:]
    return jnp.concatenate([first_half * cosine - second * sine_part, second * cosine + first_half * sine_part], axis=-1)

def attention(queries, key_rows, value_rows, seq_docs):
    length = queries.shape[0]
    block_rows = min(512, length)
    group_size = QH // KVH
    scaling = HD ** (-0.5)
    places = jnp.arange(length).astype(jnp.int32)

    def one_block(block_start):
        row_block = lax.dynamic_slice_in_dim(queries, block_start, block_rows, 0).reshape(block_rows, KVH, group_size, HD)
        row_places = lax.dynamic_slice_in_dim(places, block_start, block_rows, 0)
        row_docs = lax.dynamic_slice_in_dim(seq_docs, block_start, block_rows, 0)
        scores = low_back(jnp.einsum('qgrd,kgd->grqk', row_block, key_rows, precision=precise) * scaling)
        allowed = (places[None, :] <= row_places[:, None]) & (seq_docs[None, :] == row_docs[:, None])
        scores = jnp.where(allowed[None, None], scores, -1e+30)
        totals = jax.nn.logsumexp(scores, axis=-1, keepdims=True)
        attn_probs = low(jnp.exp(scores - totals))
        mixed_out = jnp.einsum('grqk,kgd->qgrd', attn_probs, value_rows, precision=precise)
        return mixed_out.reshape(block_rows, QH * HD)
    starts = (jnp.arange(length // block_rows) * block_rows).astype(jnp.int32)
    return lax.map(jax.checkpoint(one_block), starts).reshape(length, QH * HD)

def layer(params, sequence, seq_docs, seq_routes):
    gain_attn, w_qkv, w_out, gain_ffn, w_router, w_gate, w_up, w_down = params
    length = sequence.shape[0]
    places = jnp.arange(length).astype(jnp.int32)
    normed = low(rms_scale(sequence, gain_attn))
    projected = low_back(jnp.dot(normed, w_qkv, precision=precise))
    queries = projected[:, :QH * HD].reshape(length, QH, HD)
    key_rows = projected[:, QH * HD:(QH + KVH) * HD].reshape(length, KVH, HD)
    value_rows = low(projected[:, (QH + KVH) * HD:].reshape(length, KVH, HD))
    queries = low(rotate(queries, places, 1.0))
    key_rows = low(rotate(key_rows, places, 1.0))
    heads = low_back(low(attention(queries, key_rows, value_rows, seq_docs)))
    middle = sequence + low_back(jnp.dot(heads, w_out, precision=precise))
    normed_ffn = low(rms_scale(middle, gain_ffn))
    logits = low_back(jnp.dot(normed_ffn, w_router, precision=precise))
    chosen = jnp.take_along_axis(logits, seq_routes, axis=1)
    gate_weights = jax.nn.softmax(chosen, axis=-1)
    blocks = length // TOK_DEV
    flat_routes = seq_routes.reshape(blocks, TOK_DEV * TOP)
    one_hot = (flat_routes[:, :, None] == jnp.arange(EXPERTS).astype(jnp.int32)[None, None, :]).astype(jnp.int32)
    slot_index = lax.optimization_barrier(jnp.sum((jnp.cumsum(one_hot, axis=1) - 1) * one_hot, axis=-1))
    block_base = (jnp.arange(blocks) * CAP).astype(jnp.int32)[:, None]
    destination = (flat_routes * (blocks * CAP) + block_base + slot_index).reshape(-1)
    buffer_rows = jnp.zeros((EXPERTS * blocks * CAP, D), jnp.float32).at[destination].set(jnp.repeat(normed_ffn, TOP, axis=0))
    buffer_rows = buffer_rows.reshape(EXPERTS, blocks * CAP, D)
    gate_act = low_back(jnp.einsum('erd,edf->erf', buffer_rows, w_gate, precision=precise))
    up_act = low_back(jnp.einsum('erd,edf->erf', buffer_rows, w_up, precision=precise))
    hidden = low(jax.nn.silu(gate_act) * up_act)
    expert_out = low_back(low(jnp.einsum('erf,efd->erd', hidden, w_down, precision=precise)))
    returned = expert_out.reshape(EXPERTS * blocks * CAP, D)[destination].reshape(length, TOP, D)
    return middle + lax.optimization_barrier(jnp.sum(gate_weights[:, :, None] * returned, axis=1))

def reference(tokens, doc_ids, gain_attn, w_qkv, w_out, gain_ffn, w_router, routes, w_gate, w_up, w_down, grad_output):
    params = tuple((weight_array.astype(jnp.float32) for weight_array in (gain_attn, w_qkv, w_out, gain_ffn, w_router, w_gate, w_up, w_down)))

    def forward(inputs, weights):

        def one_sequence(batch_item):
            sequence, seq_docs, seq_routes = batch_item
            return layer(weights, sequence, seq_docs, seq_routes)
        return lax.map(jax.checkpoint(one_sequence), (inputs, doc_ids, routes))
    result, pullback = jax.vjp(forward, tokens.astype(jnp.float32), params)
    grad_inputs, grad_params = pullback(grad_output.astype(jnp.float32))
    return (result.astype(jnp.bfloat16), grad_inputs.astype(jnp.bfloat16), grad_params[0], grad_params[1], grad_params[2], grad_params[3], grad_params[4], grad_params[5], grad_params[6], grad_params[7])
```

```python
import jax
import jax.numpy as jnp
from jax import lax
from jax.experimental import pallas as pl
from jax.experimental.pallas import tpu as pltpu
from jax.sharding import PartitionSpec as P

D = 1024
FF = 512
QH = 16
KVH = 8
HD = 64
ROWS = 128
CAP = 64
BF = jnp.bfloat16
F32 = jnp.float32
VMEM_BYTES = 60 * 1024 * 1024

NN = (((1,), (0,)), ((), ()))
NT = (((1,), (1,)), ((), ()))
TN = (((0,), (0,)), ((), ()))


def mm(a, b, dims=NN):
    return lax.dot_general(a, b, dims, preferred_element_type=F32)


def shift(value, axis, by):
    size = lax.axis_size(axis)
    return lax.ppermute(value, axis, [(i, (i + by) % size) for i in range(size)])


def swap(value, axis):
    size = lax.axis_size(axis)
    return lax.ppermute(value, axis, [(i, i ^ 1) for i in range(size)])


def gather_ctx(value):
    half = value.shape[0] // 2
    up, down = shift(value, "ctx", -2), shift(value, "ctx", 2)
    far = jnp.concatenate([shift(up[:half], "ctx", -2), shift(down[half:], "ctx", 2)], axis=0)
    mine = jnp.stack([value, up, down, far])
    return jnp.concatenate([mine, swap(mine, "ctx")], axis=0)


def sum_ctx(blocks):
    half = blocks.shape[1] // 2
    summed = blocks[:4].astype(F32) + swap(blocks[4:], "ctx").astype(F32)
    far = summed[3].astype(BF)
    to_up, to_down = shift(far[:half], "ctx", 2), shift(far[half:], "ctx", -2)
    up = jnp.concatenate([summed[1, :half] + to_up.astype(F32), summed[1, half:]], axis=0)
    down = jnp.concatenate([summed[2, :half], summed[2, half:] + to_down.astype(F32)], axis=0)
    from_up, from_down = shift(up.astype(BF), "ctx", 2), shift(down.astype(BF), "ctx", -2)
    return summed[0] + from_up.astype(F32) + from_down.astype(F32)


def gather_expert(value):
    half = value.shape[0] // 2
    beside = swap(value, "expert")
    up, down = shift(value, "expert", -2), shift(value, "expert", 2)
    beside_up, beside_down = shift(beside, "expert", -2), shift(beside, "expert", 2)
    far = jnp.concatenate([shift(up[:half], "expert", -2), shift(down[half:], "expert", 2)], axis=0)
    beside_far = swap(far, "expert")
    return jnp.stack([value, beside, up, beside_up, down, beside_down, far, beside_far])


def owner_order(me):
    steps = jnp.array([0, 0, 2, 2, -2, -2, 4, 4], jnp.int32)
    flips = jnp.array([0, 1, 0, 1, 0, 1, 0, 1], jnp.int32)
    return jnp.bitwise_xor((me + steps + 8) % 8, flips)


def rms_parts(values):
    return lax.rsqrt(jnp.mean(values * values, axis=-1, keepdims=True) + 1e-06)


def rms_back(values, scale, gain, grad):
    weighted = grad * gain
    inner = jnp.mean(values * weighted, axis=-1, keepdims=True)
    return scale * weighted - values * (scale * scale * scale) * inner


def rotate(values, cosine, sine):
    half = HD // 2
    first, second = values[..., :half], values[..., half:]
    return jnp.concatenate(
        [first * cosine - second * sine, second * cosine + first * sine], axis=-1
    )


def pad_heads(values):
    split = values.reshape(ROWS, 4, 2, 2, HD)
    wide = split[:, :, :, :, None, :] * jnp.eye(2, dtype=values.dtype)[None, None, :, None, :, None]
    return jnp.transpose(wide, (1, 2, 3, 0, 4, 5)).reshape(4, 4 * ROWS, 2 * HD)


def merge_heads(parts, lane):
    low = jnp.where(lane < HD, parts[0], pltpu.roll(parts[1], HD, 1))
    high = jnp.where(lane < HD, pltpu.roll(parts[2], HD, 1), parts[3])
    return low, high


def attend_kernel(
    q_ref, kv_ref, row_ref, key_ref, w_out_ref, tok_ref, gain_ref, heads_ref, lse_ref, mid_ref, nf_ref
):
    allowed = (key_ref[0:1, :] <= row_ref[:, 0:1]) & (key_ref[1:2, :] == row_ref[:, 1:2])
    lane = lax.broadcasted_iota(jnp.int32, (ROWS, 128), 1)
    stats = jnp.zeros((ROWS, 128), F32)
    for j in range(4):
        keys = kv_ref[:, j * 128 : (j + 1) * 128]
        vals = kv_ref[:, 512 + j * 128 : 512 + (j + 1) * 128]
        parts = []
        for h in range(4):
            scores = mm(q_ref[j, h * ROWS : (h + 1) * ROWS, :], keys, NT)
            scores = jnp.where(allowed, scores, -1e30)
            top = jnp.max(scores, axis=1, keepdims=True)
            powers = jnp.exp(scores - top)
            total = jnp.sum(powers, axis=1, keepdims=True)
            stats = jnp.where(lane == 4 * j + h, top + jnp.log(total), stats)
            probs = (powers * (1.0 / total)).astype(BF)
            parts.append(mm(probs, vals))
        low, high = merge_heads(parts, lane)
        heads_ref[:, j * 256 : j * 256 + 128] = low.astype(BF)
        heads_ref[:, j * 256 + 128 : j * 256 + 256] = high.astype(BF)
    lse_ref[...] = stats
    middle = tok_ref[...].astype(F32) + mm(heads_ref[...], w_out_ref[...])
    mid_ref[...] = middle
    nf_ref[...] = (middle * rms_parts(middle) * gain_ref[...]).astype(BF)


def attend(q_pad, kv_all, row_info, key_info, w_out, tokens, gain):
    return pl.pallas_call(
        attend_kernel,
        out_shape=(
            jax.ShapeDtypeStruct((ROWS, D), BF),
            jax.ShapeDtypeStruct((ROWS, 128), F32),
            jax.ShapeDtypeStruct((ROWS, D), F32),
            jax.ShapeDtypeStruct((ROWS, D), BF),
        ),
        compiler_params=pltpu.CompilerParams(vmem_limit_bytes=VMEM_BYTES),
        name="attend",
    )(q_pad, kv_all, row_info, key_info, w_out, tokens, gain)


def attend_back_kernel(q_ref, g_ref, kv_ref, lse_ref, row_ref, key_ref, dq_ref, dkv_ref):
    allowed = (key_ref[:, 0:1] <= row_ref[0:1, :]) & (key_ref[:, 1:2] == row_ref[1:2, :])
    lane = lax.broadcasted_iota(jnp.int32, (ROWS, 128), 1)
    for j in range(4):
        keys = kv_ref[:, j * 128 : (j + 1) * 128]
        vals = kv_ref[:, 512 + j * 128 : 512 + (j + 1) * 128]
        parts = []
        grad_keys = jnp.zeros((8 * ROWS, 128), F32)
        grad_vals = jnp.zeros((8 * ROWS, 128), F32)
        for h in range(4):
            query = q_ref[j, h * ROWS : (h + 1) * ROWS, :]
            grads = g_ref[j, h * ROWS : (h + 1) * ROWS, :]
            scores = jnp.where(allowed, mm(keys, query, NT), -1e30)
            probs = jnp.exp(scores - lse_ref[4 * j + h : 4 * j + h + 1, :])
            grad_probs = mm(vals, grads, NT)
            delta = jnp.sum(probs * grad_probs, axis=0, keepdims=True)
            grad_scores = (probs * (grad_probs - delta)).astype(BF)
            grad_keys = grad_keys + mm(grad_scores, query)
            grad_vals = grad_vals + mm(probs.astype(BF), grads)
            parts.append(mm(grad_scores, keys, TN))
        low, high = merge_heads(parts, lane)
        dq_ref[:, j * 256 : j * 256 + 128] = low * (HD**-0.5)
        dq_ref[:, j * 256 + 128 : j * 256 + 256] = high * (HD**-0.5)
        dkv_ref[:, j * 128 : (j + 1) * 128] = grad_keys.astype(BF)
        dkv_ref[:, 512 + j * 128 : 512 + (j + 1) * 128] = grad_vals.astype(BF)


def attend_back(q_pad, g_pad, kv_all, lse_rows, row_info, key_info):
    return pl.pallas_call(
        attend_back_kernel,
        out_shape=(
            jax.ShapeDtypeStruct((ROWS, D), F32),
            jax.ShapeDtypeStruct((8 * ROWS, D), BF),
        ),
        compiler_params=pltpu.CompilerParams(vmem_limit_bytes=VMEM_BYTES),
        name="attend_back",
    )(q_pad, g_pad, kv_all, lse_rows, row_info, key_info)


def experts_kernel(
    order_ref,
    x_ref,
    g_ref,
    routes_ref,
    router_ref,
    w_gate_ref,
    w_up_ref,
    w_down_ref,
    out_ref,
    back_ref,
    grad_ref,
    xs,
    gs,
    sel,
    gate_rows,
    gg,
):
    e = pl.program_id(0)

    @pl.when(e == 0)
    def _():
        upper = (
            lax.broadcasted_iota(jnp.int32, (ROWS, ROWS), 0)
            <= lax.broadcasted_iota(jnp.int32, (ROWS, ROWS), 1)
        ).astype(BF)
        names = lax.broadcasted_iota(jnp.int32, (32, ROWS), 0)
        slots = lax.broadcasted_iota(jnp.int32, (CAP, ROWS), 0)

        def block(b, carry):
            routes = routes_ref[b]
            chosen = jnp.zeros((32, ROWS), F32)
            for k in range(8):
                chosen = jnp.where(names == routes[k : k + 1, :], 1.0, chosen)
            place = mm(chosen.astype(BF), upper).astype(jnp.int32) - 1
            logits = mm(router_ref[...], x_ref[b], NT)
            top = jnp.max(jnp.where(chosen > 0, logits, -3e38), axis=0, keepdims=True)
            powers = jnp.where(chosen > 0, jnp.exp(jnp.minimum(logits - top, 0.0)), 0.0)
            weights = powers / jnp.sum(powers, axis=0, keepdims=True)
            for c in range(4):
                hit = (slots == place[c : c + 1, :]) & (chosen[c : c + 1, :] > 0)
                sel[b, c * CAP : (c + 1) * CAP, :] = hit.astype(F32).astype(BF)
                gate_rows[c, b] = jnp.sum(
                    jnp.where(hit, weights[c : c + 1, :], 0.0), axis=1, keepdims=True
                )
            xs[b] = mm(sel[b], x_ref[b]).astype(BF)
            gs[b] = mm(sel[b], g_ref[b]).astype(BF)
            gg[b] = jnp.zeros((8, ROWS), F32)
            return carry

        lax.fori_loop(0, 8, block, 0)

    at = pl.ds(pl.multiple_of(e * CAP, CAP), CAP)
    rows = xs[:, at, :].reshape(8 * CAP, D)
    grads = gs[:, at, :].reshape(8 * CAP, D).astype(F32)
    weight = gate_rows[e].reshape(8 * CAP, 1)
    gate_act = mm(rows, w_gate_ref[0])
    up_act = mm(rows, w_up_ref[0])
    sig = 1.0 / (1.0 + jnp.exp(-gate_act))
    silu = gate_act * sig
    hidden = (silu * up_act).astype(BF)
    made = mm(hidden, w_down_ref[0])
    grad_gate = jnp.sum(made * grads, axis=1, keepdims=True).reshape(8, CAP, 1)
    grad_rows = (weight * grads).astype(BF)
    grad_hidden = mm(grad_rows, w_down_ref[0], NT)
    grad_gate_act = (grad_hidden * up_act * (sig * (1.0 + gate_act * (1.0 - sig)))).astype(BF)
    grad_up_act = (grad_hidden * silu).astype(BF)
    grad_ref[:, 0, 64:96, :] = mm(hidden, grad_rows, TN).astype(BF).reshape(16, 32, D)
    grad_ref[:, 0, 0:64, 0:FF] = mm(rows, grad_gate_act, TN).astype(BF).reshape(16, 64, FF)
    grad_ref[:, 0, 0:64, FF:D] = mm(rows, grad_up_act, TN).astype(BF).reshape(16, 64, FF)
    xs[:, at, :] = (weight * made).astype(BF).reshape(8, CAP, D)
    grad_x = mm(grad_gate_act, w_gate_ref[0], NT) + mm(grad_up_act, w_up_ref[0], NT)
    gs[:, at, :] = grad_x.astype(BF).reshape(8, CAP, D)
    sub = lax.broadcasted_iota(jnp.int32, (8, ROWS), 0)
    for b in range(8):
        line = jnp.sum(sel[b, at, :].astype(F32) * grad_gate[b], axis=0, keepdims=True)
        high = line.astype(BF).astype(F32)
        gg[b] = jnp.where(sub == e, high, jnp.where(sub == e + 4, line - high, gg[b]))

    @pl.when(e == 3)
    def _():
        def block(b, carry):
            to = order_ref[b]
            out_ref[to] = mm(sel[b], xs[b], TN).astype(BF)
            back_ref[to, :, 0:D] = mm(sel[b], gs[b], TN).astype(BF)
            tall = jnp.concatenate([gg[b], jnp.zeros((ROWS - 8, ROWS), F32)], axis=0)
            back_ref[to, :, D : D + 128] = tall.T.astype(BF)
            return carry

        lax.fori_loop(0, 8, block, 0)


def experts(order, rows_all, grads_all, routes_rel, router_rel, w_gate, w_up, w_down):
    whole = lambda *shape: pl.BlockSpec(shape, lambda e, order: (0,) * len(shape))
    return pl.pallas_call(
        experts_kernel,
        grid_spec=pltpu.PrefetchScalarGridSpec(
            num_scalar_prefetch=1,
            grid=(4,),
            in_specs=[
                whole(8, ROWS, D),
                whole(8, ROWS, D),
                whole(8, 8, ROWS),
                whole(32, D),
                pl.BlockSpec((1, D, FF), lambda e, order: (e, 0, 0)),
                pl.BlockSpec((1, D, FF), lambda e, order: (e, 0, 0)),
                pl.BlockSpec((1, FF, D), lambda e, order: (e, 0, 0)),
            ],
            out_specs=[
                whole(8, ROWS, D),
                whole(8, ROWS, D + 128),
                pl.BlockSpec((16, 1, 96, D), lambda e, order: (0, e, 0, 0)),
            ],
            scratch_shapes=[
                pltpu.VMEM((8, 4 * CAP, D), BF),
                pltpu.VMEM((8, 4 * CAP, D), BF),
                pltpu.VMEM((8, 4 * CAP, ROWS), BF),
                pltpu.VMEM((4, 8, CAP, 1), F32),
                pltpu.VMEM((8, 8, ROWS), F32),
            ],
        ),
        out_shape=(
            jax.ShapeDtypeStruct((8, ROWS, D), BF),
            jax.ShapeDtypeStruct((8, ROWS, D + 128), BF),
            jax.ShapeDtypeStruct((16, 4, 96, D), BF),
        ),
        compiler_params=pltpu.CompilerParams(
            dimension_semantics=("arbitrary",), vmem_limit_bytes=VMEM_BYTES
        ),
        name="experts",
    )(order, rows_all, grads_all, routes_rel, router_rel, w_gate, w_up, w_down)


def to_all(value, axis):
    return lax.all_to_all(value, axis, 0, 0, tiled=True)


def local(
    tokens,
    doc_ids,
    gain_attn,
    w_qkv,
    w_out,
    gain_ffn,
    w_router,
    routes,
    w_gate,
    w_up,
    w_down,
    grad_output,
):
    ctx = lax.axis_index("ctx")
    me = lax.axis_index("expert")
    inputs = tokens[0].astype(F32)
    grad_out = grad_output[0].astype(F32)
    gain_first = gain_attn.astype(F32)[None, :]
    gain_second = gain_ffn.astype(F32)[None, :]
    places = ctx * ROWS + jnp.arange(ROWS, dtype=jnp.int32)
    docs = doc_ids[0].reshape(8, ROWS)
    frequency = 10000.0 ** (-jnp.arange(HD // 2).astype(F32) / (HD // 2))
    angles = places.astype(F32)[:, None] * frequency[None, :]
    cosine, sine = jnp.cos(angles)[:, None, :], jnp.sin(angles)[:, None, :]

    named = jnp.pad(routes[0].astype(BF), ((0, 0), (0, 120)))
    told = gather_expert(jnp.concatenate([grad_output[0], named], axis=1))
    routes_all = jnp.transpose(told[:, :, D : D + 8].astype(jnp.int32), (0, 2, 1))
    routes_rel = (routes_all - 4 * me + 32) % 32
    router_rel = jnp.roll(w_router, -4 * me, axis=1).T

    first_scale = rms_parts(inputs)
    normed = (inputs * first_scale * gain_first).astype(BF)
    normed_all = lax.all_gather(normed, "expert", axis=0, tiled=True)
    projected = mm(normed, w_qkv)
    queries = rotate(projected[:, : QH * HD].reshape(ROWS, QH, HD), cosine, sine)
    q_pad = pad_heads((queries.astype(BF) * (HD**-0.5)).astype(BF))
    key_own = rotate(
        projected[:, QH * HD : (QH + KVH) * HD].reshape(ROWS, KVH, HD), cosine, sine
    ).reshape(ROWS, KVH * HD)
    kv_own = jnp.concatenate([key_own, projected[:, (QH + KVH) * HD :]], axis=1).astype(BF)
    kv_all = gather_ctx(kv_own).reshape(8 * ROWS, D)
    ring = jnp.array([0, 2, -2, 4], jnp.int32)
    block_ids = jnp.concatenate([ctx + ring, jnp.bitwise_xor(ctx, 1) + ring]) % 8
    picks = (block_ids[:, None] == jnp.arange(8)[None, :]).astype(jnp.int32)
    key_docs = jnp.sum(picks[:, :, None] * docs[None], axis=1).reshape(-1)
    key_places = (block_ids[:, None] * ROWS + jnp.arange(ROWS)[None, :]).reshape(-1)
    own_docs = jnp.sum((jnp.arange(8) == ctx).astype(jnp.int32)[:, None] * docs, axis=0)
    row_info = jnp.stack([places, own_docs])
    key_info = jnp.stack([key_places, key_docs]).astype(jnp.int32)

    heads, lse, middle, normed_ffn = attend(
        q_pad, kv_all, row_info.T, key_info, w_out, tokens[0], gain_second
    )
    rows_all = gather_expert(normed_ffn)
    heads_all = to_all(jnp.broadcast_to(heads[None], (8, ROWS, D)), "expert").reshape(-1, D)
    made, back, grad_experts = experts(
        owner_order(me), rows_all, told[:, :, :D], routes_rel, router_rel, w_gate, w_up, w_down
    )
    back = to_all(back, "expert")
    made = to_all(made, "expert")
    expert_sums = lax.psum_scatter(grad_experts.reshape(16 * 4 * 96, D), ("dp", "ctx"), tiled=True)
    output = (middle + jnp.sum(made.astype(F32), axis=0)).astype(BF)

    logits = mm(normed_ffn, w_router)
    chosen = jnp.any(routes[0][:, :, None] == jnp.arange(32)[None, None, :], axis=1)
    gates = jax.nn.softmax(jnp.where(chosen, logits, -jnp.inf), axis=-1)
    tails = back[:, :, D : D + 8].astype(F32)
    grad_gates = jnp.transpose(tails[:, :, :4] + tails[:, :, 4:], (1, 0, 2)).reshape(ROWS, 32)
    grad_logits = (
        gates * (grad_gates - jnp.sum(gates * grad_gates, axis=-1, keepdims=True))
    ).astype(BF)
    grad_router = mm(normed_ffn, grad_logits, TN)
    grad_normed_ffn = jnp.sum(back[:, :, :D].astype(F32), axis=0) + mm(grad_logits, w_router, NT)
    second_scale = rms_parts(middle)
    grad_gain_second = jnp.sum(grad_normed_ffn * middle * second_scale, axis=0)
    grad_middle = grad_out + rms_back(middle, second_scale, gain_second, grad_normed_ffn)
    grad_branch = grad_middle.astype(BF)
    grad_heads = mm(grad_branch, w_out, NT).astype(BF)
    branch_cols = to_all(
        jnp.transpose(grad_branch.reshape(ROWS, 8, 128), (1, 0, 2)), "expert"
    ).reshape(8 * ROWS, 128)
    grad_out_cols = mm(heads_all, branch_cols, TN)

    grad_q, grad_kv = attend_back(
        q_pad, pad_heads(grad_heads), kv_all, lse[:, :QH].T, row_info, key_info.T
    )
    grad_kv = sum_ctx(grad_kv.reshape(8, ROWS, D))
    grad_q = rotate(grad_q.reshape(ROWS, QH, HD), cosine, -sine).reshape(ROWS, QH * HD)
    grad_k = rotate(grad_kv[:, : KVH * HD].reshape(ROWS, KVH, HD), cosine, -sine)
    grad_mixed = jnp.concatenate(
        [grad_q, grad_k.reshape(ROWS, KVH * HD), grad_kv[:, KVH * HD :]], axis=1
    ).astype(BF)
    mixed_cols = to_all(
        jnp.transpose(grad_mixed.reshape(ROWS, 8, 256), (1, 0, 2)), "expert"
    ).reshape(8 * ROWS, 256)
    grad_qkv_cols = mm(normed_all, mixed_cols, TN)
    grad_normed = mm(grad_mixed, w_qkv, NT)
    grad_gain_first = jnp.sum(grad_normed * inputs * first_scale, axis=0)
    grad_tokens = grad_middle + rms_back(inputs, first_scale, gain_first, grad_normed)

    dense = jnp.concatenate(
        [
            grad_qkv_cols,
            grad_out_cols,
            grad_router,
            grad_gain_first[:, None],
            grad_gain_second[:, None],
            jnp.zeros((D, 94), F32),
        ],
        axis=1,
    ).astype(BF)
    dense = jnp.sum(to_all(dense.reshape(16, 64, 512), ("dp", "ctx")).astype(F32), axis=0)
    dense = to_all(dense.astype(BF).reshape(8, 8, 512), "expert").astype(F32)
    rest = jnp.sum(dense[:, :, 384:], axis=0)
    parts = expert_sums.reshape(4, 96, D).astype(F32)
    return (
        output[None],
        grad_tokens.astype(BF)[None],
        rest[:, 32],
        jnp.transpose(dense[:, :, :256], (1, 0, 2)).reshape(8, 2 * D),
        jnp.transpose(dense[:, :, 256:384], (1, 0, 2)).reshape(8, D),
        rest[:, 33],
        rest[:, :32],
        parts[:, :64, :FF],
        parts[:, :64, FF:],
        parts[:, 64:, :],
    )


def solution(mesh):
    in_specs = (
        P(("dp", "expert"), "ctx", None),
        P(("dp", "expert"), None),
        P(),
        P(),
        P(),
        P(),
        P(),
        P(("dp", "expert"), "ctx", None),
        P("expert", None, None),
        P("expert", None, None),
        P("expert", None, None),
        P(("dp", "expert"), "ctx", None),
    )
    out_specs = (
        P(("dp", "expert"), "ctx", None),
        P(("dp", "expert"), "ctx", None),
        P(("dp", "ctx", "expert")),
        P(("dp", "ctx", "expert"), None),
        P(("dp", "ctx", "expert"), None),
        P(("dp", "ctx", "expert")),
        P(("dp", "ctx", "expert"), None),
        P("expert", ("dp", "ctx"), None),
        P("expert", ("dp", "ctx"), None),
        P("expert", ("dp", "ctx"), None),
    )
    return jax.shard_map(local, mesh=mesh, in_specs=in_specs, out_specs=out_specs, check_vma=False)
```

```python
import functools

import jax
import jax.numpy as jnp
from jax import lax
from jax.experimental import pallas as pl
from jax.experimental.pallas import tpu as pltpu
from jax.sharding import PartitionSpec as P

D = 1024
FF = 512
QH = 16
KVH = 8
HD = 64
ROWS = 128
CAP = 64
TILE = 128
WIDE = D + TILE
ACTS = 2 * D + FF + D
BF = jnp.bfloat16
F32 = jnp.float32
VMEM_BYTES = 60 * 1024 * 1024

NN = (((1,), (0,)), ((), ()))
NT = (((1,), (1,)), ((), ()))
TN = (((0,), (0,)), ((), ()))


def mm(a, b, dims=NN):
    return lax.dot_general(a, b, dims, preferred_element_type=F32)


def send(value, axis, to):
    return lax.ppermute(value, axis, [(i, to(i)) for i in range(lax.axis_size(axis))])


def up(i):
    return (i + 2) % 8


def down(i):
    return (i - 2) % 8


def far(i):
    return (i + 4) % 8


def beside(i):
    return i ^ 1


def kernel_call(body, name, out_shape, **more):
    return pl.pallas_call(
        body,
        out_shape=out_shape,
        compiler_params=pltpu.CompilerParams(vmem_limit_bytes=VMEM_BYTES),
        name=name,
        **more,
    )


def shaped(dtype, *shape):
    return jax.ShapeDtypeStruct(shape, dtype)


def lanes(rows=ROWS):
    return lax.broadcasted_iota(jnp.int32, (rows, TILE), 1)


def rms_parts(values):
    return lax.rsqrt(jnp.mean(values * values, axis=-1, keepdims=True) + 1e-06)


def rms_back(values, scale, gain, grad):
    weighted = grad * gain
    inner = jnp.mean(values * weighted, axis=-1, keepdims=True)
    return scale * weighted - values * (scale * scale * scale) * inner


def partner(tile, lane):
    return jnp.where(lane % HD < HD // 2, pltpu.roll(tile, TILE - 32, 1), pltpu.roll(tile, 32, 1))


def put_padded(ref, t, tile, lane):
    turned = pltpu.roll(tile, HD, 1)
    j, g = t // 2, t % 2
    own = (lane < HD) if g == 0 else (lane >= HD)
    first, second = (tile, turned) if g == 0 else (turned, tile)
    at = 2 * g * ROWS
    ref[j, at : at + ROWS, :] = jnp.where(own, first, 0.0).astype(BF)
    ref[j, at + ROWS : at + 2 * ROWS, :] = jnp.where(own, second, 0.0).astype(BF)


def merge_heads(parts, lane):
    low = jnp.where(lane < HD, parts[0], pltpu.roll(parts[1], HD, 1))
    high = jnp.where(lane < HD, pltpu.roll(parts[2], HD, 1), parts[3])
    return low, high


def column_sums(values):
    high = values.astype(BF)
    low = (values - high.astype(F32)).astype(BF)
    ones = jnp.ones((ROWS, TILE), BF)
    return mm(high, ones, TN) + mm(low, ones, TN)


def first_kernel(tok_ref, gain_ref, w_ref, cos_ref, sin_ref, normed_ref, q_ref, kv_ref):
    values = tok_ref[...].astype(F32)
    normed = (values * rms_parts(values) * gain_ref[...]).astype(BF)
    normed_ref[...] = normed
    lane = lanes()
    cosine, sine = cos_ref[...], sin_ref[...]
    for t in range(16):
        tile = mm(normed, w_ref[:, t * TILE : (t + 1) * TILE])
        if t < 12:
            tile = tile * cosine + partner(tile, lane) * sine
        if t < 8:
            put_padded(q_ref, t, tile.astype(BF).astype(F32) * (HD**-0.5), lane)
        else:
            kv_ref[:, (t - 8) * TILE : (t - 7) * TILE] = tile.astype(BF)


def fill_keys(kv, own_ref, beside_ref, mine_ref, other_ref):
    kv[0:ROWS] = own_ref[...]
    kv[4 * ROWS : 5 * ROWS] = beside_ref[...]
    for k in range(3):
        kv[(k + 1) * ROWS : (k + 2) * ROWS] = mine_ref[k]
        kv[(k + 5) * ROWS : (k + 6) * ROWS] = other_ref[k]


def attend_kernel(
    q_ref,
    own_ref,
    beside_ref,
    mine_ref,
    other_ref,
    row_ref,
    key_ref,
    w_out_ref,
    tok_ref,
    gain_ref,
    heads_ref,
    lse_ref,
    mid_ref,
    nf_ref,
    kv,
):
    fill_keys(kv, own_ref, beside_ref, mine_ref, other_ref)
    allowed = (key_ref[0:1, :] <= row_ref[:, 0:1]) & (key_ref[1:2, :] == row_ref[:, 1:2])
    lane = lanes()
    stats = jnp.zeros((ROWS, TILE), F32)
    for j in range(4):
        keys = kv[:, j * 128 : (j + 1) * 128]
        vals = kv[:, 512 + j * 128 : 512 + (j + 1) * 128]
        parts = []
        for h in range(4):
            scores = mm(q_ref[j, h * ROWS : (h + 1) * ROWS, :], keys, NT)
            scores = jnp.where(allowed, scores, -1e30)
            top = jnp.max(scores, axis=1, keepdims=True)
            powers = jnp.exp(scores - top)
            total = jnp.sum(powers, axis=1, keepdims=True)
            stats = jnp.where(lane == 4 * j + h, top + jnp.log(total), stats)
            probs = (powers * (1.0 / total)).astype(BF)
            parts.append(mm(probs, vals))
        low, high = merge_heads(parts, lane)
        heads_ref[:, j * 256 : j * 256 + 128] = low.astype(BF)
        heads_ref[:, j * 256 + 128 : j * 256 + 256] = high.astype(BF)
    lse_ref[...] = stats.T
    middle = tok_ref[...].astype(F32) + mm(heads_ref[...], w_out_ref[...])
    mid_ref[...] = middle
    nf_ref[...] = (middle * rms_parts(middle) * gain_ref[...]).astype(BF)


def middle_kernel(
    backs,
    nf_ref,
    mid_ref,
    gout_ref,
    gain_ref,
    routes_ref,
    router_ref,
    w_out_ref,
    gmid_ref,
    rest_ref,
    g_pad,
    cols_ref,
):
    lane = lanes()
    total = jnp.zeros((ROWS, D), F32)
    grad_gates = jnp.zeros((ROWS, TILE), F32)
    for r in range(8):
        total = total + backs[r, :, 0:D].astype(F32)
        tail = backs[r, :, D:WIDE].astype(F32)
        tail = jnp.where(lane < 4, tail + pltpu.roll(tail, TILE - 4, 1), 0.0)
        grad_gates = grad_gates + (pltpu.roll(tail, 4 * r, 1) if r else tail)
    chosen = lane < 0
    for k in range(8):
        chosen = chosen | (lane == routes_ref[:, k : k + 1])
    logits = mm(nf_ref[...], router_ref[...])
    top = jnp.max(jnp.where(chosen, logits, -3e38), axis=1, keepdims=True)
    powers = jnp.where(chosen, jnp.exp(jnp.minimum(logits - top, 0.0)), 0.0)
    gates = powers / jnp.sum(powers, axis=1, keepdims=True)
    mean = jnp.sum(gates * grad_gates, axis=1, keepdims=True)
    grad_logits = (gates * (grad_gates - mean)).astype(BF)
    total = total + mm(grad_logits, router_ref[...], NT)
    middle = mid_ref[...]
    scale = rms_parts(middle)
    gain_column = column_sums(total * middle * scale)
    router_part = mm(nf_ref[...], grad_logits, TN)
    rest_ref[...] = jnp.where(lanes(D) == 33, gain_column, router_part)
    grad_middle = gout_ref[...].astype(F32) + rms_back(middle, scale, gain_ref[...], total)
    gmid_ref[...] = grad_middle
    branch = grad_middle.astype(BF)
    for t in range(8):
        cols_ref[t] = branch[:, t * TILE : (t + 1) * TILE]
        tile = mm(branch, w_out_ref[t * TILE : (t + 1) * TILE, :], NT)
        put_padded(g_pad, t, tile, lane)


def back_kernel(
    g_pad,
    q_ref,
    own_ref,
    beside_ref,
    mine_ref,
    other_ref,
    lse_ref,
    row_ref,
    key_ref,
    cos_ref,
    sin_ref,
    branch_ref,
    after_0_ref,
    after_1_ref,
    after_2_ref,
    cols_ref,
    gq_ref,
    dkv_mine_ref,
    dkv_other_ref,
    kv,
):
    fill_keys(kv, own_ref, beside_ref, mine_ref, other_ref)
    lane = lanes()
    allowed = (key_ref[:, 0:1] <= row_ref[0:1, :]) & (key_ref[:, 1:2] == row_ref[1:2, :])
    cosine, sine = cos_ref[...], sin_ref[...]
    for j in range(4):
        keys = kv[:, j * 128 : (j + 1) * 128]
        vals = kv[:, 512 + j * 128 : 512 + (j + 1) * 128]
        parts = []
        grad_keys = jnp.zeros((8 * ROWS, 128), F32)
        grad_vals = jnp.zeros((8 * ROWS, 128), F32)
        for h in range(4):
            query = q_ref[j, h * ROWS : (h + 1) * ROWS, :]
            grads = g_pad[j, h * ROWS : (h + 1) * ROWS, :]
            scores = jnp.where(allowed, mm(keys, query, NT), -1e30)
            probs = jnp.exp(scores - lse_ref[4 * j + h : 4 * j + h + 1, :])
            grad_probs = mm(vals, grads, NT)
            delta = jnp.sum(probs * grad_probs, axis=0, keepdims=True)
            grad_scores = (probs * (grad_probs - delta)).astype(BF)
            grad_keys = grad_keys + mm(grad_scores, query)
            grad_vals = grad_vals + mm(probs.astype(BF), grads)
            parts.append(mm(grad_scores, keys, TN))
        for g, tile in enumerate(merge_heads(parts, lane)):
            tile = tile * (HD**-0.5)
            tile = (tile * cosine - partner(tile, lane) * sine).astype(BF)
            t = 2 * j + g
            cols_ref[t, :, 0:TILE] = branch_ref[t]
            cols_ref[t, :, TILE : 2 * TILE] = tile
            gq_ref[:, t * TILE : (t + 1) * TILE] = tile
        for ref, at in ((dkv_mine_ref, 0), (dkv_other_ref, 4)):
            for k in range(4):
                rows = slice((at + k) * ROWS, (at + k + 1) * ROWS)
                ref[k, :, j * 128 : (j + 1) * 128] = grad_keys[rows].astype(BF)
                ref[k, :, 512 + j * 128 : 512 + (j + 1) * 128] = grad_vals[rows].astype(BF)


def turn_kernel(own_ref, a_ref, b_ref, c_ref, cos_ref, sin_ref, early_ref, *refs):
    cols_ref = refs[-1]
    lane = lanes()
    for t in range(8):
        at = slice(t * TILE, (t + 1) * TILE)
        tile = own_ref[:, at] + a_ref[:, at].astype(F32)
        tile = tile + b_ref[:, at].astype(F32) + c_ref[:, at].astype(F32)
        if t < 4:
            tile = tile * cos_ref[...] - partner(tile, lane) * sin_ref[...]
        cols_ref[t, :, 0 : 2 * TILE] = early_ref[t]
        cols_ref[t, :, 2 * TILE : 3 * TILE] = tile.astype(BF)


def last_kernel(gq_ref, cols_ref, w_ref, tok_ref, gain_ref, gmid_ref, rest_ref, gtok_ref, side_ref):
    grad = mm(gq_ref[...], w_ref[:, 0:D], NT)
    for t in range(8):
        grad = grad + mm(cols_ref[t, :, 2 * TILE : 3 * TILE], w_ref[:, D + t * TILE : D + (t + 1) * TILE], NT)
    values = tok_ref[...].astype(F32)
    scale = rms_parts(values)
    column = column_sums(grad * values * scale)
    side_ref[...] = jnp.where(lanes(D) == 32, column, rest_ref[...]).astype(BF)
    grad_values = gmid_ref[...] + rms_back(values, scale, gain_ref[...], grad)
    gtok_ref[...] = grad_values.astype(BF)


def experts_kernel(order_ref, *refs):
    blocks, refs = refs[:8], refs[8:]
    told_ref, router_ref, wg_ref, wu_ref, wd_ref, made_ref, back_ref, keep_ref, give_ref = refs[:9]
    xs, gs, sel, gate_rows, gg, grad_ref = refs[9:]
    e = pl.program_id(0)
    count = 8 * CAP

    @pl.when(e == 0)
    def _():
        upper = (
            lax.broadcasted_iota(jnp.int32, (ROWS, ROWS), 0)
            <= lax.broadcasted_iota(jnp.int32, (ROWS, ROWS), 1)
        ).astype(BF)
        names = (lax.broadcasted_iota(jnp.int32, (32, ROWS), 0) + 4 * order_ref[8]) % 32
        slots = lax.broadcasted_iota(jnp.int32, (CAP, ROWS), 0)
        for b in range(8):
            told = told_ref[order_ref[b]]
            routes = told[:, D:WIDE].astype(F32).T[0:8].astype(jnp.int32)
            chosen = jnp.zeros((32, ROWS), F32)
            for k in range(8):
                chosen = jnp.where(names == routes[k : k + 1, :], 1.0, chosen)
            place = mm(chosen.astype(BF), upper).astype(jnp.int32) - 1
            logits = mm(router_ref[...], blocks[b][...], NT)
            top = jnp.max(jnp.where(chosen > 0, logits, -3e38), axis=0, keepdims=True)
            powers = jnp.where(chosen > 0, jnp.exp(jnp.minimum(logits - top, 0.0)), 0.0)
            weights = powers / jnp.sum(powers, axis=0, keepdims=True)
            for c in range(4):
                hit = (slots == place[c : c + 1, :]) & (chosen[c : c + 1, :] > 0)
                sel[b, c * CAP : (c + 1) * CAP, :] = hit.astype(F32).astype(BF)
                gate_rows[c, b] = jnp.sum(
                    jnp.where(hit, weights[c : c + 1, :], 0.0), axis=1, keepdims=True
                )
            xs[b] = mm(sel[b], blocks[b][...]).astype(BF)
            gs[b] = mm(sel[b], told[:, 0:D]).astype(BF)
            gg[b] = jnp.zeros((8, ROWS), F32)

    at = pl.ds(pl.multiple_of(e * CAP, CAP), CAP)
    rows = xs[:, at, :].reshape(count, D)
    grads = gs[:, at, :].reshape(count, D).astype(F32)
    weight = gate_rows[e].reshape(count, 1)
    gate_act = mm(rows, wg_ref[0])
    up_act = mm(rows, wu_ref[0])
    sig = 1.0 / (1.0 + jnp.exp(-gate_act))
    silu = gate_act * sig
    hidden = (silu * up_act).astype(BF)
    made = mm(hidden, wd_ref[0])
    grad_gate = jnp.sum(made * grads, axis=1, keepdims=True).reshape(8, CAP, 1)
    grad_rows = (weight * grads).astype(BF)
    grad_hidden = mm(grad_rows, wd_ref[0], NT)
    grad_gate_act = (grad_hidden * up_act * (sig * (1.0 + gate_act * (1.0 - sig)))).astype(BF)
    grad_up_act = (grad_hidden * silu).astype(BF)
    grad_ref[:, 64:96, :] = mm(hidden, grad_rows, TN).astype(BF).reshape(16, 32, D)
    joint = mm(rows, jnp.concatenate([grad_gate_act, grad_up_act], axis=1), TN)
    grad_ref[:, 0:64, :] = joint.astype(BF).reshape(16, 64, D)
    for c, ref in enumerate((keep_ref, give_ref)):
        for d in range(2):
            for z in range(4):
                ring = (order_ref[10] + z) % 4
                ref[d, z, 0] = grad_ref[(order_ref[9] ^ d) * 8 + ring * 2 + (order_ref[11] ^ c)]
    xs[:, at, :] = (weight * made).astype(BF).reshape(8, CAP, D)
    grad_x = mm(grad_gate_act, wg_ref[0], NT) + mm(grad_up_act, wu_ref[0], NT)
    gs[:, at, :] = grad_x.astype(BF).reshape(8, CAP, D)
    sub = lax.broadcasted_iota(jnp.int32, (8, ROWS), 0)
    for b in range(8):
        line = jnp.sum(sel[b, at, :].astype(F32) * grad_gate[b], axis=0, keepdims=True)
        high = line.astype(BF).astype(F32)
        gg[b] = jnp.where(sub == e, high, jnp.where(sub == e + 4, line - high, gg[b]))

    @pl.when(e == 3)
    def _():
        for b in range(8):
            to = order_ref[b]
            made_ref[to] = mm(sel[b], xs[b], TN).astype(BF)
            back_ref[to, :, 0:D] = mm(sel[b], gs[b], TN).astype(BF)
            tall = jnp.concatenate([gg[b], jnp.zeros((ROWS - 8, ROWS), F32)], axis=0)
            back_ref[to, :, D:WIDE] = tall.T.astype(BF)


def experts(order, blocks, told, router_rel, w_gate, w_up, w_down):
    whole = lambda *shape: pl.BlockSpec(shape, lambda e, order: (0,) * len(shape))
    return pl.pallas_call(
        experts_kernel,
        grid_spec=pltpu.PrefetchScalarGridSpec(
            num_scalar_prefetch=1,
            grid=(4,),
            in_specs=[whole(ROWS, D)] * 8
            + [
                whole(8, ROWS, WIDE),
                whole(32, D),
                pl.BlockSpec((1, D, FF), lambda e, order: (e, 0, 0)),
                pl.BlockSpec((1, D, FF), lambda e, order: (e, 0, 0)),
                pl.BlockSpec((1, FF, D), lambda e, order: (e, 0, 0)),
            ],
            out_specs=[
                whole(8, ROWS, D),
                whole(8, ROWS, WIDE),
                pl.BlockSpec((2, 4, 1, 96, D), lambda e, order: (0, 0, e, 0, 0)),
                pl.BlockSpec((2, 4, 1, 96, D), lambda e, order: (0, 0, e, 0, 0)),
            ],
            scratch_shapes=[
                pltpu.VMEM((8, 4 * CAP, D), BF),
                pltpu.VMEM((8, 4 * CAP, D), BF),
                pltpu.VMEM((8, 4 * CAP, ROWS), BF),
                pltpu.VMEM((4, 8, CAP, 1), F32),
                pltpu.VMEM((8, 8, ROWS), F32),
                pltpu.VMEM((16, 96, D), BF),
            ],
        ),
        out_shape=[
            shaped(BF, 8, ROWS, D),
            shaped(BF, 8, ROWS, WIDE),
            shaped(BF, 2, 4, 4, 96, D),
            shaped(BF, 2, 4, 4, 96, D),
        ],
        compiler_params=pltpu.CompilerParams(
            dimension_semantics=("arbitrary",), vmem_limit_bytes=VMEM_BYTES
        ),
        name="experts",
    )(order, *blocks, told, router_rel, w_gate, w_up, w_down)


ANY = pl.BlockSpec(memory_space=pl.ANY)


def hold_kernel(value_ref, after_ref, out_ref):
    out_ref[...] = value_ref[...]


def join_x_kernel(keep_ref, got_ref, *refs):
    for d in range(2):
        both = keep_ref[d, 0].astype(F32) + got_ref[d, 0].astype(F32)
        refs[d - 2][0] = both.astype(BF)


def join_x(keep, got, start, after):
    block = pl.BlockSpec((2, 1, 2, 96, D), lambda z: (0, z, start // 2, 0, 0))
    return kernel_call(
        join_x_kernel,
        "join_x",
        [shaped(BF, 4, 2, 96, D)] * 2,
        grid=(4,),
        in_specs=[block, block] + [ANY] * len(after),
        out_specs=[pl.BlockSpec((1, 2, 96, D), lambda z: (z, 0, 0, 0))] * 2,
    )(keep, got, *after)


def join_rings_kernel(keep_ref, got_ref, *refs):
    for z in range(4):
        both = keep_ref[0, z, 0].astype(F32) + got_ref[0, z, 0].astype(F32)
        refs[z - 4][0, 0] = both.astype(BF)


def sum_z_first(keep, got, start):
    block = pl.BlockSpec((1, 4, 1, 96, D), lambda d, e: (d, 0, start + e, 0, 0))
    here, ahead, across, behind = kernel_call(
        join_rings_kernel,
        "join_rings",
        [shaped(BF, 2, 2, 96, D)] * 4,
        grid=(2, 2),
        in_specs=[block, block],
        out_specs=[pl.BlockSpec((1, 1, 96, D), lambda d, e: (d, e, 0, 0))] * 4,
    )(keep, got)
    came = [send(ahead, "ctx", up), send(behind, "ctx", down), send(across, "ctx", far)]
    half = lambda d: here[d].astype(F32) + sum(v[d].astype(F32) for v in came)
    return half(0) + send(half(1).astype(BF), "dp", beside).astype(F32), came, here


def join_z_kernel(own_ref, got_ref, *refs):
    for z in range(4):
        refs[z - 4][0] = (own_ref[z, 0].astype(F32) + got_ref[z, 0].astype(F32)).astype(BF)


def sum_z(own, got, after):
    block = pl.BlockSpec((4, 1, 96, D), lambda e: (0, e, 0, 0))
    here, ahead, across, behind = kernel_call(
        join_z_kernel,
        "join_z",
        [shaped(BF, 2, 96, D)] * 4,
        grid=(2,),
        in_specs=[block, block] + [ANY] * len(after),
        out_specs=[pl.BlockSpec((1, 96, D), lambda e: (e, 0, 0))] * 4,
    )(own, got, *after)
    came = [send(ahead, "ctx", up), send(behind, "ctx", down), send(across, "ctx", far)]
    return here.astype(F32) + sum(v.astype(F32) for v in came), came


def join_kv_kernel(mine_ref, got_ref, *refs):
    own, outs = refs[-4], refs[-3:]
    own[...] = mine_ref[0].astype(F32) + got_ref[0].astype(F32)
    for k in range(3):
        outs[k][...] = (mine_ref[k + 1].astype(F32) + got_ref[k + 1].astype(F32)).astype(BF)


def to_all(value, axis):
    return lax.all_to_all(value, axis, 0, 0, tiled=True)


def local(
    tokens,
    doc_ids,
    gain_attn,
    w_qkv,
    w_out,
    gain_ffn,
    w_router,
    routes,
    w_gate,
    w_up,
    w_down,
    grad_output,
):
    vmem = pl.BlockSpec(memory_space=pltpu.VMEM)
    ctx = lax.axis_index("ctx")
    me = lax.axis_index("expert")
    gain_first = gain_attn.astype(F32)[None, :]
    gain_second = gain_ffn.astype(F32)[None, :]

    named = jnp.pad(routes[0].astype(BF), ((0, 0), (0, TILE - 8)))
    told = jnp.concatenate([grad_output[0], named], axis=1)
    told = lax.all_gather(told, "expert", axis=0)

    places = ctx * ROWS + jnp.arange(ROWS, dtype=jnp.int32)
    lane = jnp.arange(TILE)
    frequency = 10000.0 ** (-(lane % 32).astype(F32) / (HD // 2))
    angles = places.astype(F32)[:, None] * frequency[None, :]
    cosine = jnp.cos(angles)
    sine = jnp.sin(angles) * jnp.where(lane % HD < HD // 2, -1.0, 1.0)[None, :]
    normed, q_pad, kv_own = kernel_call(
        first_kernel,
        "project",
        (shaped(BF, ROWS, D), shaped(BF, 4, 4 * ROWS, TILE), shaped(BF, ROWS, D)),
    )(tokens[0], gain_first, w_qkv, cosine, sine)

    normed_all = lax.all_gather(normed, "expert", axis=0, tiled=True)
    kv_mine = [send(kv_own, "ctx", to) for to in (down, up, far)]
    kv_beside = send(kv_own, "ctx", beside)
    kv_mine = jnp.stack(kv_mine)
    kv_other = send(kv_mine, "ctx", beside)
    keys = (kv_own, kv_beside, kv_mine, kv_other)

    docs = doc_ids[0].reshape(8, ROWS)
    ring = jnp.array([0, 2, -2, 4], jnp.int32)
    block_ids = jnp.concatenate([ctx + ring, jnp.bitwise_xor(ctx, 1) + ring]) % 8
    picks = (block_ids[:, None] == jnp.arange(8)[None, :]).astype(jnp.int32)
    key_docs = jnp.sum(picks[:, :, None] * docs[None], axis=1).reshape(-1)
    key_places = (block_ids[:, None] * ROWS + jnp.arange(ROWS)[None, :]).reshape(-1)
    own_docs = jnp.sum((jnp.arange(8) == ctx).astype(jnp.int32)[:, None] * docs, axis=0)
    row_info = jnp.stack([places, own_docs])
    key_info = jnp.stack([key_places, key_docs]).astype(jnp.int32)

    heads, lse, middle, normed_ffn = kernel_call(
        attend_kernel,
        "attend",
        (
            shaped(BF, ROWS, D),
            shaped(F32, ROWS, TILE),
            shaped(F32, ROWS, D),
            shaped(BF, ROWS, D),
        ),
        scratch_shapes=[pltpu.VMEM((8 * ROWS, D), BF)],
    )(q_pad, *keys, row_info.T, key_info, w_out, tokens[0], gain_second)

    heads_all = lax.all_gather(heads, "expert", axis=0, tiled=True)

    from_up, from_down, from_far = (send(normed_ffn, "expert", to) for to in (down, up, far))
    from_beside = send(normed_ffn, "expert", beside)
    other_up, other_down, other_far = (send(from_beside, "expert", to) for to in (down, up, far))
    router_rel = jnp.roll(w_router, -4 * me, axis=1).T
    pair = jnp.bitwise_xor(me, 1)
    order = [me, pair, up(me), (me + 6) % 8, far(me), up(pair), (pair + 6) % 8, far(pair), me]
    order += [lax.axis_index("dp"), ctx // 2, ctx % 2]
    blocks = (normed_ffn, from_beside, from_up, from_down)
    blocks += (from_far, other_up, other_down, other_far)
    made, back, keep, give = experts(
        jnp.stack(order).astype(jnp.int32), blocks, told, router_rel, w_gate, w_up, w_down
    )
    back = to_all(back, "expert")
    given = send(give, "ctx", beside)
    own_0, other_0 = join_x(keep, given, 0, [])
    crossed_0 = send(other_0, "dp", beside)
    sums_1, came_1, own_1 = sum_z_first(keep, given, 2)
    made = kernel_call(hold_kernel, "hold", shaped(BF, 8, ROWS, D), in_specs=[vmem, ANY])(made, back)
    made = to_all(made, "expert")

    router_wide = jnp.pad(w_router, ((0, 0), (0, TILE - 32)))
    operands = (
        back,
        normed_ffn,
        middle,
        grad_output[0],
        gain_second,
        routes[0],
        router_wide,
        w_out,
    )
    grad_middle, rest, g_pad, branch = kernel_call(
        middle_kernel,
        "middle_back",
        (
            shaped(F32, ROWS, D),
            shaped(F32, D, TILE),
            shaped(BF, 4, 4 * ROWS, TILE),
            shaped(BF, 8, ROWS, TILE),
        ),
        in_specs=[vmem] * len(operands),
    )(*operands)
    cols, grad_q, dkv_mine, dkv_other = kernel_call(
        back_kernel,
        "attend_back",
        (
            shaped(BF, 8, ROWS, 2 * TILE),
            shaped(BF, ROWS, D),
            shaped(BF, 4, ROWS, D),
            shaped(BF, 4, ROWS, D),
        ),
        in_specs=[vmem] * 12 + [ANY] * 3,
        scratch_shapes=[pltpu.VMEM((8 * ROWS, D), BF)],
    )(g_pad, q_pad, *keys, lse, row_info, key_info.T, cosine, sine, branch, *came_1)

    own, *parts = kernel_call(
        join_kv_kernel,
        "join_kv",
        [shaped(F32, ROWS, D)] + [shaped(BF, ROWS, D)] * 3,
        in_specs=[vmem] * 2 + [ANY],
    )(dkv_mine, send(dkv_other, "ctx", beside), crossed_0)
    arrived = [send(v, "ctx", to) for v, to in zip(parts, (up, down, far))]
    sums_0, came_0 = sum_z(own_0, crossed_0, [])
    cols = kernel_call(
        turn_kernel, "turn", shaped(BF, 8, ROWS, 3 * TILE), in_specs=[vmem] * 7 + [ANY] * 4
    )(own, *arrived, cosine, sine, cols, *came_0, made)
    here = to_all(cols, "expert")
    here = here.reshape(8 * ROWS, 3 * TILE)
    grad_tokens, side = kernel_call(
        last_kernel, "grad_tokens", (shaped(BF, ROWS, D), shaped(BF, D, TILE))
    )(grad_q, cols, w_qkv, tokens[0], gain_first, grad_middle, rest)
    output = (middle + jnp.sum(made.astype(F32), axis=0)).astype(BF)

    out_cols = mm(heads_all, here[:, :TILE], TN).astype(BF)
    mixed_cols = mm(normed_all, here[:, TILE:], TN).astype(BF)
    dense = jnp.concatenate([mixed_cols, out_cols, side], axis=1)
    dense = jnp.sum(to_all(dense.reshape(16, 64, 4 * TILE), ("dp", "ctx")).astype(F32), axis=0)
    dense = to_all(dense.astype(BF).reshape(8, 8, 4 * TILE), "expert").astype(F32)
    tiles = jnp.transpose(dense[:, :, : 3 * TILE].reshape(8, 8, 3, TILE), (1, 2, 0, 3))
    rest = jnp.sum(dense[:, :, 3 * TILE :], axis=0)
    parts = jnp.concatenate([sums_0, sums_1], axis=0)
    return (
        output[None],
        grad_tokens[None],
        rest[:, 32],
        tiles[:, :2].reshape(8, 2 * D),
        tiles[:, 2].reshape(8, D),
        rest[:, 33],
        rest[:, :32],
        parts[:, :64, :FF],
        parts[:, :64, FF:],
        parts[:, 64:, :],
    )


def solution(mesh):
    in_specs = (
        P(("dp", "expert"), "ctx", None),
        P(("dp", "expert"), None),
        P(),
        P(),
        P(),
        P(),
        P(),
        P(("dp", "expert"), "ctx", None),
        P("expert", None, None),
        P("expert", None, None),
        P("expert", None, None),
        P(("dp", "expert"), "ctx", None),
    )
    out_specs = (
        P(("dp", "expert"), "ctx", None),
        P(("dp", "expert"), "ctx", None),
        P(("dp", "ctx", "expert")),
        P(("dp", "ctx", "expert"), None),
        P(("dp", "ctx", "expert"), None),
        P(("dp", "ctx", "expert")),
        P(("dp", "ctx", "expert"), None),
        P("expert", ("dp", "ctx"), None),
        P("expert", ("dp", "ctx"), None),
        P("expert", ("dp", "ctx"), None),
    )
    return jax.shard_map(local, mesh=mesh, in_specs=in_specs, out_specs=out_specs, check_vma=False)
```

```python
import functools

import jax
import jax.numpy as jnp
from jax import lax
from jax.experimental import pallas as pl
from jax.experimental.pallas import tpu as pltpu
from jax.sharding import PartitionSpec as P

D = 1024
FF = 512
QH = 16
KVH = 8
HD = 64
ROWS = 128
CAP = 64
TILE = 128
WIDE = D + TILE
BF = jnp.bfloat16
F32 = jnp.float32
VMEM_BYTES = 60 * 1024 * 1024

NN = (((1,), (0,)), ((), ()))
NT = (((1,), (1,)), ((), ()))
TN = (((0,), (0,)), ((), ()))


def mm(a, b, dims=NN):
    return lax.dot_general(a, b, dims, preferred_element_type=F32)


def send(value, axis, to):
    return lax.ppermute(value, axis, [(i, to(i)) for i in range(lax.axis_size(axis))])


def up(i):
    return (i + 2) % 8


def down(i):
    return (i - 2) % 8


def far(i):
    return (i + 4) % 8


def beside(i):
    return i ^ 1


def kernel_call(body, name, out_shape, **more):
    return pl.pallas_call(
        body,
        out_shape=out_shape,
        compiler_params=pltpu.CompilerParams(vmem_limit_bytes=VMEM_BYTES),
        name=name,
        **more,
    )


def shaped(dtype, *shape):
    return jax.ShapeDtypeStruct(shape, dtype)


def lanes(rows=ROWS):
    return lax.broadcasted_iota(jnp.int32, (rows, TILE), 1)


def rms_parts(values):
    return lax.rsqrt(jnp.mean(values * values, axis=-1, keepdims=True) + 1e-06)


def rms_back(values, scale, gain, grad):
    weighted = grad * gain
    inner = jnp.mean(values * weighted, axis=-1, keepdims=True)
    return scale * weighted - values * (scale * scale * scale) * inner


def partner(tile, lane):
    return jnp.where(lane % HD < HD // 2, pltpu.roll(tile, TILE - 32, 1), pltpu.roll(tile, 32, 1))


def put_padded(ref, t, tile, lane):
    turned = pltpu.roll(tile, HD, 1)
    j, g = t // 2, t % 2
    own = (lane < HD) if g == 0 else (lane >= HD)
    first, second = (tile, turned) if g == 0 else (turned, tile)
    at = 2 * g * ROWS
    ref[j, at : at + ROWS, :] = jnp.where(own, first, 0.0).astype(BF)
    ref[j, at + ROWS : at + 2 * ROWS, :] = jnp.where(own, second, 0.0).astype(BF)


def merge_heads(parts, lane):
    low = jnp.where(lane < HD, parts[0], pltpu.roll(parts[1], HD, 1))
    high = jnp.where(lane < HD, pltpu.roll(parts[2], HD, 1), parts[3])
    return low, high


def column_sums(values):
    high = values.astype(BF)
    low = (values - high.astype(F32)).astype(BF)
    ones = jnp.ones((ROWS, TILE), BF)
    return mm(high, ones, TN) + mm(low, ones, TN)


def first_kernel(tok_ref, gain_ref, w_ref, cos_ref, sin_ref, normed_ref, q_ref, kv_ref):
    values = tok_ref[...].astype(F32)
    normed = (values * rms_parts(values) * gain_ref[...]).astype(BF)
    normed_ref[...] = normed
    lane = lanes()
    cosine, sine = cos_ref[...], sin_ref[...]
    for t in range(16):
        tile = mm(normed, w_ref[:, t * TILE : (t + 1) * TILE])
        if t < 12:
            tile = tile * cosine + partner(tile, lane) * sine
        if t < 8:
            put_padded(q_ref, t, tile.astype(BF).astype(F32) * (HD**-0.5), lane)
        else:
            kv_ref[:, (t - 8) * TILE : (t - 7) * TILE] = tile.astype(BF)


def fill_keys(kv, own_ref, beside_ref, mine_ref, other_ref):
    kv[0:ROWS] = own_ref[...]
    kv[4 * ROWS : 5 * ROWS] = beside_ref[...]
    for k in range(3):
        kv[(k + 1) * ROWS : (k + 2) * ROWS] = mine_ref[k]
        kv[(k + 5) * ROWS : (k + 6) * ROWS] = other_ref[k]


def attend_kernel(
    q_ref,
    own_ref,
    beside_ref,
    mine_ref,
    other_ref,
    row_ref,
    key_ref,
    w_out_ref,
    tok_ref,
    gain_ref,
    heads_ref,
    lse_ref,
    mid_ref,
    nf_ref,
    kv,
):
    fill_keys(kv, own_ref, beside_ref, mine_ref, other_ref)
    allowed = (key_ref[0:1, :] <= row_ref[:, 0:1]) & (key_ref[1:2, :] == row_ref[:, 1:2])
    lane = lanes()
    stats = jnp.zeros((ROWS, TILE), F32)
    for j in range(4):
        keys = kv[:, j * 128 : (j + 1) * 128]
        vals = kv[:, 512 + j * 128 : 512 + (j + 1) * 128]
        parts = []
        for h in range(4):
            scores = mm(q_ref[j, h * ROWS : (h + 1) * ROWS, :], keys, NT)
            scores = jnp.where(allowed, scores, -1e30)
            top = jnp.max(scores, axis=1, keepdims=True)
            powers = jnp.exp(scores - top)
            total = jnp.sum(powers, axis=1, keepdims=True)
            stats = jnp.where(lane == 4 * j + h, top + jnp.log(total), stats)
            probs = (powers * (1.0 / total)).astype(BF)
            parts.append(mm(probs, vals))
        low, high = merge_heads(parts, lane)
        heads_ref[:, j * 256 : j * 256 + 128] = low.astype(BF)
        heads_ref[:, j * 256 + 128 : j * 256 + 256] = high.astype(BF)
    lse_ref[...] = stats.T
    middle = tok_ref[...].astype(F32) + mm(heads_ref[...], w_out_ref[...])
    mid_ref[...] = middle
    nf_ref[...] = (middle * rms_parts(middle) * gain_ref[...]).astype(BF)


def middle_kernel(
    backs,
    nf_ref,
    mid_ref,
    gout_ref,
    gain_ref,
    routes_ref,
    router_ref,
    w_out_ref,
    gmid_ref,
    rest_ref,
    g_pad,
    cols_ref,
):
    lane = lanes()
    total = jnp.zeros((ROWS, D), F32)
    grad_gates = jnp.zeros((ROWS, TILE), F32)
    for r in range(8):
        total = total + backs[r, :, 0:D].astype(F32)
        tail = backs[r, :, D:WIDE].astype(F32)
        tail = jnp.where(lane < 4, tail + pltpu.roll(tail, TILE - 4, 1), 0.0)
        grad_gates = grad_gates + (pltpu.roll(tail, 4 * r, 1) if r else tail)
    chosen = lane < 0
    for k in range(8):
        chosen = chosen | (lane == routes_ref[:, k : k + 1])
    logits = mm(nf_ref[...], router_ref[...])
    top = jnp.max(jnp.where(chosen, logits, -3e38), axis=1, keepdims=True)
    powers = jnp.where(chosen, jnp.exp(jnp.minimum(logits - top, 0.0)), 0.0)
    gates = powers / jnp.sum(powers, axis=1, keepdims=True)
    mean = jnp.sum(gates * grad_gates, axis=1, keepdims=True)
    grad_logits = (gates * (grad_gates - mean)).astype(BF)
    total = total + mm(grad_logits, router_ref[...], NT)
    middle = mid_ref[...]
    scale = rms_parts(middle)
    gain_column = column_sums(total * middle * scale)
    router_part = mm(nf_ref[...], grad_logits, TN)
    rest_ref[...] = jnp.where(lanes(D) == 33, gain_column, router_part)
    grad_middle = gout_ref[...].astype(F32) + rms_back(middle, scale, gain_ref[...], total)
    gmid_ref[...] = grad_middle
    branch = grad_middle.astype(BF)
    for t in range(8):
        cols_ref[t] = branch[:, t * TILE : (t + 1) * TILE]
        tile = mm(branch, w_out_ref[t * TILE : (t + 1) * TILE, :], NT)
        put_padded(g_pad, t, tile, lane)


def back_kernel(
    g_pad,
    q_ref,
    own_ref,
    beside_ref,
    mine_ref,
    other_ref,
    lse_ref,
    row_ref,
    key_ref,
    cos_ref,
    sin_ref,
    branch_ref,
    after_0_ref,
    after_1_ref,
    after_2_ref,
    cols_ref,
    gq_ref,
    dkv_mine_ref,
    dkv_other_ref,
    kv,
):
    fill_keys(kv, own_ref, beside_ref, mine_ref, other_ref)
    lane = lanes()
    allowed = (key_ref[:, 0:1] <= row_ref[0:1, :]) & (key_ref[:, 1:2] == row_ref[1:2, :])
    cosine, sine = cos_ref[...], sin_ref[...]
    for j in range(4):
        keys = kv[:, j * 128 : (j + 1) * 128]
        vals = kv[:, 512 + j * 128 : 512 + (j + 1) * 128]
        parts = []
        grad_keys = jnp.zeros((8 * ROWS, 128), F32)
        grad_vals = jnp.zeros((8 * ROWS, 128), F32)
        for h in range(4):
            query = q_ref[j, h * ROWS : (h + 1) * ROWS, :]
            grads = g_pad[j, h * ROWS : (h + 1) * ROWS, :]
            scores = jnp.where(allowed, mm(keys, query, NT), -1e30)
            probs = jnp.exp(scores - lse_ref[4 * j + h : 4 * j + h + 1, :])
            grad_probs = mm(vals, grads, NT)
            delta = jnp.sum(probs * grad_probs, axis=0, keepdims=True)
            grad_scores = (probs * (grad_probs - delta)).astype(BF)
            grad_keys = grad_keys + mm(grad_scores, query)
            grad_vals = grad_vals + mm(probs.astype(BF), grads)
            parts.append(mm(grad_scores, keys, TN))
        for g, tile in enumerate(merge_heads(parts, lane)):
            tile = tile * (HD**-0.5)
            tile = (tile * cosine - partner(tile, lane) * sine).astype(BF)
            t = 2 * j + g
            cols_ref[t, :, 0:TILE] = branch_ref[t]
            cols_ref[t, :, TILE : 2 * TILE] = tile
            gq_ref[:, t * TILE : (t + 1) * TILE] = tile
        for ref, at in ((dkv_mine_ref, 0), (dkv_other_ref, 4)):
            for k in range(4):
                rows = slice((at + k) * ROWS, (at + k + 1) * ROWS)
                ref[k, :, j * 128 : (j + 1) * 128] = grad_keys[rows].astype(BF)
                ref[k, :, 512 + j * 128 : 512 + (j + 1) * 128] = grad_vals[rows].astype(BF)


def turn_kernel(own_ref, a_ref, b_ref, c_ref, cos_ref, sin_ref, early_ref, *refs):
    cols_ref = refs[-1]
    lane = lanes()
    for t in range(8):
        at = slice(t * TILE, (t + 1) * TILE)
        tile = own_ref[:, at] + a_ref[:, at].astype(F32)
        tile = tile + b_ref[:, at].astype(F32) + c_ref[:, at].astype(F32)
        if t < 4:
            tile = tile * cos_ref[...] - partner(tile, lane) * sin_ref[...]
        cols_ref[t, :, 0 : 2 * TILE] = early_ref[t]
        cols_ref[t, :, 2 * TILE : 3 * TILE] = tile.astype(BF)


def last_kernel(gq_ref, cols_ref, w_ref, tok_ref, gain_ref, gmid_ref, rest_ref, *refs):
    gtok_ref, side_ref = refs[-2:]
    grad = mm(gq_ref[...], w_ref[:, 0:D], NT)
    for t in range(8):
        grad = grad + mm(cols_ref[t, :, 2 * TILE : 3 * TILE], w_ref[:, D + t * TILE : D + (t + 1) * TILE], NT)
    values = tok_ref[...].astype(F32)
    scale = rms_parts(values)
    column = column_sums(grad * values * scale)
    side_ref[...] = jnp.where(lanes(D) == 32, column, rest_ref[...]).astype(BF)
    grad_values = gmid_ref[...] + rms_back(values, scale, gain_ref[...], grad)
    gtok_ref[...] = grad_values.astype(BF)


def experts_kernel(order_ref, *refs):
    blocks, refs = refs[:8], refs[8:]
    told_ref, router_ref, wg_ref, wu_ref, wd_ref, made_ref, back_ref, keep_ref, give_ref = refs[:9]
    xs, gs, sel, gate_rows, gg, grad_ref = refs[9:]
    e = pl.program_id(0)
    count = 8 * CAP

    @pl.when(e == 0)
    def _():
        upper = (
            lax.broadcasted_iota(jnp.int32, (ROWS, ROWS), 0)
            <= lax.broadcasted_iota(jnp.int32, (ROWS, ROWS), 1)
        ).astype(BF)
        names = (lax.broadcasted_iota(jnp.int32, (32, ROWS), 0) + 4 * order_ref[8]) % 32
        slots = lax.broadcasted_iota(jnp.int32, (CAP, ROWS), 0)
        for b in range(8):
            told = told_ref[order_ref[b]]
            routes = told[:, D:WIDE].astype(F32).T[0:8].astype(jnp.int32)
            chosen = jnp.zeros((32, ROWS), F32)
            for k in range(8):
                chosen = jnp.where(names == routes[k : k + 1, :], 1.0, chosen)
            place = mm(chosen.astype(BF), upper).astype(jnp.int32) - 1
            logits = mm(router_ref[...], blocks[b][...], NT)
            top = jnp.max(jnp.where(chosen > 0, logits, -3e38), axis=0, keepdims=True)
            powers = jnp.where(chosen > 0, jnp.exp(jnp.minimum(logits - top, 0.0)), 0.0)
            weights = powers / jnp.sum(powers, axis=0, keepdims=True)
            for c in range(4):
                hit = (slots == place[c : c + 1, :]) & (chosen[c : c + 1, :] > 0)
                sel[b, c * CAP : (c + 1) * CAP, :] = hit.astype(F32).astype(BF)
                gate_rows[c, b] = jnp.sum(
                    jnp.where(hit, weights[c : c + 1, :], 0.0), axis=1, keepdims=True
                )
            xs[b] = mm(sel[b], blocks[b][...]).astype(BF)
            gs[b] = mm(sel[b], told[:, 0:D]).astype(BF)
            gg[b] = jnp.zeros((8, ROWS), F32)

    at = pl.ds(pl.multiple_of(e * CAP, CAP), CAP)
    rows = xs[:, at, :].reshape(count, D)
    grads = gs[:, at, :].reshape(count, D).astype(F32)
    weight = gate_rows[e].reshape(count, 1)
    gate_act = mm(rows, wg_ref[0])
    up_act = mm(rows, wu_ref[0])
    sig = 1.0 / (1.0 + jnp.exp(-gate_act))
    silu = gate_act * sig
    hidden = (silu * up_act).astype(BF)
    made = mm(hidden, wd_ref[0])
    grad_gate = jnp.sum(made * grads, axis=1, keepdims=True).reshape(8, CAP, 1)
    grad_rows = (weight * grads).astype(BF)
    grad_hidden = mm(grad_rows, wd_ref[0], NT)
    grad_gate_act = (grad_hidden * up_act * (sig * (1.0 + gate_act * (1.0 - sig)))).astype(BF)
    grad_up_act = (grad_hidden * silu).astype(BF)
    grad_ref[:, 64:96, :] = mm(hidden, grad_rows, TN).astype(BF).reshape(16, 32, D)
    joint = mm(rows, jnp.concatenate([grad_gate_act, grad_up_act], axis=1), TN)
    grad_ref[:, 0:64, :] = joint.astype(BF).reshape(16, 64, D)
    for c, ref in enumerate((keep_ref, give_ref)):
        for d in range(2):
            for z in range(4):
                ring = (order_ref[10] + z) % 4
                ref[d, z, 0] = grad_ref[(order_ref[9] ^ d) * 8 + ring * 2 + (order_ref[11] ^ c)]
    xs[:, at, :] = (weight * made).astype(BF).reshape(8, CAP, D)
    grad_x = mm(grad_gate_act, wg_ref[0], NT) + mm(grad_up_act, wu_ref[0], NT)
    gs[:, at, :] = grad_x.astype(BF).reshape(8, CAP, D)
    sub = lax.broadcasted_iota(jnp.int32, (8, ROWS), 0)
    for b in range(8):
        line = jnp.sum(sel[b, at, :].astype(F32) * grad_gate[b], axis=0, keepdims=True)
        high = line.astype(BF).astype(F32)
        gg[b] = jnp.where(sub == e, high, jnp.where(sub == e + 4, line - high, gg[b]))

    @pl.when(e == 3)
    def _():
        for b in range(8):
            to = order_ref[b]
            made_ref[to] = mm(sel[b], xs[b], TN).astype(BF)
            back_ref[to, :, 0:D] = mm(sel[b], gs[b], TN).astype(BF)
            tall = jnp.concatenate([gg[b], jnp.zeros((ROWS - 8, ROWS), F32)], axis=0)
            back_ref[to, :, D:WIDE] = tall.T.astype(BF)


def experts(order, blocks, told, router_rel, w_gate, w_up, w_down):
    whole = lambda *shape: pl.BlockSpec(shape, lambda e, order: (0,) * len(shape))
    return pl.pallas_call(
        experts_kernel,
        grid_spec=pltpu.PrefetchScalarGridSpec(
            num_scalar_prefetch=1,
            grid=(4,),
            in_specs=[whole(ROWS, D)] * 8
            + [
                whole(8, ROWS, WIDE),
                whole(32, D),
                pl.BlockSpec((1, D, FF), lambda e, order: (e, 0, 0)),
                pl.BlockSpec((1, D, FF), lambda e, order: (e, 0, 0)),
                pl.BlockSpec((1, FF, D), lambda e, order: (e, 0, 0)),
            ],
            out_specs=[
                whole(8, ROWS, D),
                whole(8, ROWS, WIDE),
                pl.BlockSpec((2, 4, 1, 96, D), lambda e, order: (0, 0, e, 0, 0)),
                pl.BlockSpec((2, 4, 1, 96, D), lambda e, order: (0, 0, e, 0, 0)),
            ],
            scratch_shapes=[
                pltpu.VMEM((8, 4 * CAP, D), BF),
                pltpu.VMEM((8, 4 * CAP, D), BF),
                pltpu.VMEM((8, 4 * CAP, ROWS), BF),
                pltpu.VMEM((4, 8, CAP, 1), F32),
                pltpu.VMEM((8, 8, ROWS), F32),
                pltpu.VMEM((16, 96, D), BF),
            ],
        ),
        out_shape=[
            shaped(BF, 8, ROWS, D),
            shaped(BF, 8, ROWS, WIDE),
            shaped(BF, 2, 4, 4, 96, D),
            shaped(BF, 2, 4, 4, 96, D),
        ],
        compiler_params=pltpu.CompilerParams(
            dimension_semantics=("arbitrary",), vmem_limit_bytes=VMEM_BYTES
        ),
        name="experts",
    )(order, *blocks, told, router_rel, w_gate, w_up, w_down)


ANY = pl.BlockSpec(memory_space=pl.ANY)


def hold_kernel(value_ref, after_ref, out_ref):
    out_ref[...] = value_ref[...]


def join_x_kernel(keep_ref, got_ref, *refs):
    for d in range(2):
        both = keep_ref[d, 0].astype(F32) + got_ref[d, 0].astype(F32)
        refs[d - 2][0] = both.astype(BF)


def join_x(keep, got, start, after):
    block = pl.BlockSpec((2, 1, 2, 96, D), lambda z: (0, z, start // 2, 0, 0))
    return kernel_call(
        join_x_kernel,
        "join_x",
        [shaped(BF, 4, 2, 96, D)] * 2,
        grid=(4,),
        in_specs=[block, block] + [ANY] * len(after),
        out_specs=[pl.BlockSpec((1, 2, 96, D), lambda z: (z, 0, 0, 0))] * 2,
    )(keep, got, *after)


def join_rings_kernel(keep_ref, got_ref, *refs):
    for z in range(4):
        both = keep_ref[0, z, 0].astype(F32) + got_ref[0, z, 0].astype(F32)
        refs[z - 4][0, 0] = both.astype(BF)


def sum_z_first(keep, got, start):
    block = pl.BlockSpec((1, 4, 1, 96, D), lambda d, e: (d, 0, start + e, 0, 0))
    here, ahead, across, behind = kernel_call(
        join_rings_kernel,
        "join_rings",
        [shaped(BF, 2, 2, 96, D)] * 4,
        grid=(2, 2),
        in_specs=[block, block],
        out_specs=[pl.BlockSpec((1, 1, 96, D), lambda d, e: (d, e, 0, 0))] * 4,
    )(keep, got)
    came = [send(ahead, "ctx", up), send(behind, "ctx", down), send(across, "ctx", far)]
    half = lambda d: here[d].astype(F32) + sum(v[d].astype(F32) for v in came)
    return half(0) + send(half(1).astype(BF), "dp", beside).astype(F32), came, here


def join_z_kernel(own_ref, got_ref, *refs):
    for z in range(4):
        refs[z - 4][0] = (own_ref[z, 0].astype(F32) + got_ref[z, 0].astype(F32)).astype(BF)


def sum_z(own, got, after):
    block = pl.BlockSpec((4, 1, 96, D), lambda e: (0, e, 0, 0))
    here, ahead, across, behind = kernel_call(
        join_z_kernel,
        "join_z",
        [shaped(BF, 2, 96, D)] * 4,
        grid=(2,),
        in_specs=[block, block] + [ANY] * len(after),
        out_specs=[pl.BlockSpec((1, 96, D), lambda e: (e, 0, 0))] * 4,
    )(own, got, *after)
    came = [send(ahead, "ctx", up), send(behind, "ctx", down), send(across, "ctx", far)]
    return here.astype(F32) + sum(v.astype(F32) for v in came), came, here


def join_kv_kernel(mine_ref, got_ref, *refs):
    own, outs = refs[-4], refs[-3:]
    own[...] = mine_ref[0].astype(F32) + got_ref[0].astype(F32)
    for k in range(3):
        outs[k][...] = (mine_ref[k + 1].astype(F32) + got_ref[k + 1].astype(F32)).astype(BF)


def to_all(value, axis):
    return lax.all_to_all(value, axis, 0, 0, tiled=True)


def local(
    tokens,
    doc_ids,
    gain_attn,
    w_qkv,
    w_out,
    gain_ffn,
    w_router,
    routes,
    w_gate,
    w_up,
    w_down,
    grad_output,
):
    vmem = pl.BlockSpec(memory_space=pltpu.VMEM)
    ctx = lax.axis_index("ctx")
    me = lax.axis_index("expert")
    gain_first = gain_attn.astype(F32)[None, :]
    gain_second = gain_ffn.astype(F32)[None, :]

    named = jnp.pad(routes[0].astype(BF), ((0, 0), (0, TILE - 8)))
    told = jnp.concatenate([grad_output[0], named], axis=1)
    told = lax.all_gather(told, "expert", axis=0)

    places = ctx * ROWS + jnp.arange(ROWS, dtype=jnp.int32)
    lane = jnp.arange(TILE)
    frequency = 10000.0 ** (-(lane % 32).astype(F32) / (HD // 2))
    angles = places.astype(F32)[:, None] * frequency[None, :]
    cosine = jnp.cos(angles)
    sine = jnp.sin(angles) * jnp.where(lane % HD < HD // 2, -1.0, 1.0)[None, :]
    normed, q_pad, kv_own = kernel_call(
        first_kernel,
        "project",
        (shaped(BF, ROWS, D), shaped(BF, 4, 4 * ROWS, TILE), shaped(BF, ROWS, D)),
    )(tokens[0], gain_first, w_qkv, cosine, sine)

    normed_all = lax.all_gather(normed, "expert", axis=0, tiled=True)
    kv_mine = [send(kv_own, "ctx", to) for to in (down, up, far)]
    kv_beside = send(kv_own, "ctx", beside)
    kv_mine = jnp.stack(kv_mine)
    kv_other = send(kv_mine, "ctx", beside)
    keys = (kv_own, kv_beside, kv_mine, kv_other)

    docs = doc_ids[0].reshape(8, ROWS)
    ring = jnp.array([0, 2, -2, 4], jnp.int32)
    block_ids = jnp.concatenate([ctx + ring, jnp.bitwise_xor(ctx, 1) + ring]) % 8
    picks = (block_ids[:, None] == jnp.arange(8)[None, :]).astype(jnp.int32)
    key_docs = jnp.sum(picks[:, :, None] * docs[None], axis=1).reshape(-1)
    key_places = (block_ids[:, None] * ROWS + jnp.arange(ROWS)[None, :]).reshape(-1)
    own_docs = jnp.sum((jnp.arange(8) == ctx).astype(jnp.int32)[:, None] * docs, axis=0)
    row_info = jnp.stack([places, own_docs])
    key_info = jnp.stack([key_places, key_docs]).astype(jnp.int32)

    heads, lse, middle, normed_ffn = kernel_call(
        attend_kernel,
        "attend",
        (
            shaped(BF, ROWS, D),
            shaped(F32, ROWS, TILE),
            shaped(F32, ROWS, D),
            shaped(BF, ROWS, D),
        ),
        scratch_shapes=[pltpu.VMEM((8 * ROWS, D), BF)],
    )(q_pad, *keys, row_info.T, key_info, w_out, tokens[0], gain_second)

    heads_all = lax.all_gather(heads, "expert", axis=0, tiled=True)

    from_up, from_down, from_far = (send(normed_ffn, "expert", to) for to in (down, up, far))
    from_beside = send(normed_ffn, "expert", beside)
    other_up, other_down = (send(from_beside, "expert", to) for to in (down, up))
    other_far = send(from_far, "expert", beside)
    router_rel = jnp.roll(w_router, -4 * me, axis=1).T
    pair = jnp.bitwise_xor(me, 1)
    order = [me, pair, up(me), (me + 6) % 8, far(me), up(pair), (pair + 6) % 8, far(pair), me]
    order += [lax.axis_index("dp"), ctx // 2, ctx % 2]
    blocks = (normed_ffn, from_beside, from_up, from_down)
    blocks += (from_far, other_up, other_down, other_far)
    made, back, keep, give = experts(
        jnp.stack(order).astype(jnp.int32), blocks, told, router_rel, w_gate, w_up, w_down
    )
    back = to_all(back, "expert")
    given = send(give, "ctx", beside)
    own_0, other_0 = join_x(keep, given, 0, [])
    crossed_0 = send(other_0, "dp", beside)
    sums_1, came_1, own_1 = sum_z_first(keep, given, 2)
    made = kernel_call(hold_kernel, "hold", shaped(BF, 8, ROWS, D), in_specs=[vmem, ANY])(made, back)
    made = to_all(made, "expert")

    router_wide = jnp.pad(w_router, ((0, 0), (0, TILE - 32)))
    operands = (
        back,
        normed_ffn,
        middle,
        grad_output[0],
        gain_second,
        routes[0],
        router_wide,
        w_out,
    )
    grad_middle, rest, g_pad, branch = kernel_call(
        middle_kernel,
        "middle_back",
        (
            shaped(F32, ROWS, D),
            shaped(F32, D, TILE),
            shaped(BF, 4, 4 * ROWS, TILE),
            shaped(BF, 8, ROWS, TILE),
        ),
        in_specs=[vmem] * len(operands),
    )(*operands)
    cols, grad_q, dkv_mine, dkv_other = kernel_call(
        back_kernel,
        "attend_back",
        (
            shaped(BF, 8, ROWS, 2 * TILE),
            shaped(BF, ROWS, D),
            shaped(BF, 4, ROWS, D),
            shaped(BF, 4, ROWS, D),
        ),
        in_specs=[vmem] * 12 + [ANY] * 3,
        scratch_shapes=[pltpu.VMEM((8 * ROWS, D), BF)],
    )(g_pad, q_pad, *keys, lse, row_info, key_info.T, cosine, sine, branch, *came_1)

    own, *parts = kernel_call(
        join_kv_kernel,
        "join_kv",
        [shaped(F32, ROWS, D)] + [shaped(BF, ROWS, D)] * 3,
    )(dkv_mine, send(dkv_other, "ctx", beside))
    arrived = [send(v, "ctx", to) for v, to in zip(parts, (up, down, far))]
    sums_0, came_0, here_0 = sum_z(own_0, crossed_0, [own])
    cols = kernel_call(
        turn_kernel, "turn", shaped(BF, 8, ROWS, 3 * TILE), in_specs=[vmem] * 7 + [ANY] * 2
    )(own, *arrived, cosine, sine, cols, made, here_0)
    here = to_all(cols, "expert")
    here = here.reshape(8 * ROWS, 3 * TILE)
    grad_tokens, side = kernel_call(
        last_kernel,
        "grad_tokens",
        (shaped(BF, ROWS, D), shaped(BF, D, TILE)),
        in_specs=[vmem] * 7 + [ANY] * 3,
    )(grad_q, cols, w_qkv, tokens[0], gain_first, grad_middle, rest, *came_0)
    output = (middle + jnp.sum(made.astype(F32), axis=0)).astype(BF)

    out_cols = mm(heads_all, here[:, :TILE], TN).astype(BF)
    mixed_cols = mm(normed_all, here[:, TILE:], TN).astype(BF)
    dense = jnp.concatenate([mixed_cols, out_cols, side], axis=1)
    dense = jnp.sum(to_all(dense.reshape(16, 64, 4 * TILE), ("dp", "ctx")).astype(F32), axis=0)
    dense = to_all(dense.astype(BF).reshape(8, 8, 4 * TILE), "expert").astype(F32)
    tiles = jnp.transpose(dense[:, :, : 3 * TILE].reshape(8, 8, 3, TILE), (1, 2, 0, 3))
    rest = jnp.sum(dense[:, :, 3 * TILE :], axis=0)
    parts = jnp.concatenate([sums_0, sums_1], axis=0)
    return (
        output[None],
        grad_tokens[None],
        rest[:, 32],
        tiles[:, :2].reshape(8, 2 * D),
        tiles[:, 2].reshape(8, D),
        rest[:, 33],
        rest[:, :32],
        parts[:, :64, :FF],
        parts[:, :64, FF:],
        parts[:, 64:, :],
    )


def solution(mesh):
    in_specs = (
        P(("dp", "expert"), "ctx", None),
        P(("dp", "expert"), None),
        P(),
        P(),
        P(),
        P(),
        P(),
        P(("dp", "expert"), "ctx", None),
        P("expert", None, None),
        P("expert", None, None),
        P("expert", None, None),
        P(("dp", "expert"), "ctx", None),
    )
    out_specs = (
        P(("dp", "expert"), "ctx", None),
        P(("dp", "expert"), "ctx", None),
        P(("dp", "ctx", "expert")),
        P(("dp", "ctx", "expert"), None),
        P(("dp", "ctx", "expert"), None),
        P(("dp", "ctx", "expert")),
        P(("dp", "ctx", "expert"), None),
        P("expert", ("dp", "ctx"), None),
        P("expert", ("dp", "ctx"), None),
        P("expert", ("dp", "ctx"), None),
    )
    return jax.shard_map(local, mesh=mesh, in_specs=in_specs, out_specs=out_specs, check_vma=False)
```

```python
import functools

import jax
import jax.numpy as jnp
from jax import lax
from jax.experimental import pallas as pl
from jax.experimental.pallas import tpu as pltpu
from jax.sharding import PartitionSpec as P

D = 1024
FF = 512
QH = 16
KVH = 8
HD = 64
ROWS = 128
CAP = 64
TILE = 128
WIDE = D + TILE
BF = jnp.bfloat16
F32 = jnp.float32
VMEM_BYTES = 60 * 1024 * 1024

NN = (((1,), (0,)), ((), ()))
NT = (((1,), (1,)), ((), ()))
TN = (((0,), (0,)), ((), ()))


def mm(a, b, dims=NN):
    return lax.dot_general(a, b, dims, preferred_element_type=F32)


def send(value, axis, to):
    return lax.ppermute(value, axis, [(i, to(i)) for i in range(lax.axis_size(axis))])


def up(i):
    return (i + 2) % 8


def down(i):
    return (i - 2) % 8


def far(i):
    return (i + 4) % 8


def beside(i):
    return i ^ 1


def kernel_call(body, name, out_shape, **more):
    return pl.pallas_call(
        body,
        out_shape=out_shape,
        compiler_params=pltpu.CompilerParams(vmem_limit_bytes=VMEM_BYTES),
        name=name,
        **more,
    )


def shaped(dtype, *shape):
    return jax.ShapeDtypeStruct(shape, dtype)


def lanes(rows=ROWS):
    return lax.broadcasted_iota(jnp.int32, (rows, TILE), 1)


def rms_parts(values):
    return lax.rsqrt(jnp.mean(values * values, axis=-1, keepdims=True) + 1e-06)


def rms_back(values, scale, gain, grad):
    weighted = grad * gain
    inner = jnp.mean(values * weighted, axis=-1, keepdims=True)
    return scale * weighted - values * (scale * scale * scale) * inner


def partner(tile, lane):
    return jnp.where(lane % HD < HD // 2, pltpu.roll(tile, TILE - 32, 1), pltpu.roll(tile, 32, 1))


def put_padded(ref, t, tile, lane):
    turned = pltpu.roll(tile, HD, 1)
    j, g = t // 2, t % 2
    own = (lane < HD) if g == 0 else (lane >= HD)
    first, second = (tile, turned) if g == 0 else (turned, tile)
    at = 2 * g * ROWS
    ref[j, at : at + ROWS, :] = jnp.where(own, first, 0.0).astype(BF)
    ref[j, at + ROWS : at + 2 * ROWS, :] = jnp.where(own, second, 0.0).astype(BF)


def merge_heads(parts, lane):
    low = jnp.where(lane < HD, parts[0], pltpu.roll(parts[1], HD, 1))
    high = jnp.where(lane < HD, pltpu.roll(parts[2], HD, 1), parts[3])
    return low, high


def column_sums(values):
    high = values.astype(BF)
    low = (values - high.astype(F32)).astype(BF)
    ones = jnp.ones((ROWS, TILE), BF)
    return mm(high, ones, TN) + mm(low, ones, TN)


def first_kernel(tok_ref, gain_ref, w_ref, cos_ref, sin_ref, normed_ref, q_ref, kv_ref):
    values = tok_ref[...].astype(F32)
    normed = (values * rms_parts(values) * gain_ref[...]).astype(BF)
    normed_ref[...] = normed
    lane = lanes()
    cosine, sine = cos_ref[...], sin_ref[...]
    for t in range(16):
        tile = mm(normed, w_ref[:, t * TILE : (t + 1) * TILE])
        if t < 12:
            tile = tile * cosine + partner(tile, lane) * sine
        if t < 8:
            put_padded(q_ref, t, tile.astype(BF).astype(F32) * (HD**-0.5), lane)
        else:
            kv_ref[:, (t - 8) * TILE : (t - 7) * TILE] = tile.astype(BF)


def fill_keys(kv, own_ref, beside_ref, mine_ref, other_ref):
    kv[0:ROWS] = own_ref[...]
    kv[4 * ROWS : 5 * ROWS] = beside_ref[...]
    for k in range(3):
        kv[(k + 1) * ROWS : (k + 2) * ROWS] = mine_ref[k]
        kv[(k + 5) * ROWS : (k + 6) * ROWS] = other_ref[k]


def attend_kernel(
    q_ref,
    own_ref,
    beside_ref,
    mine_ref,
    other_ref,
    row_ref,
    key_ref,
    w_out_ref,
    tok_ref,
    gain_ref,
    heads_ref,
    lse_ref,
    mid_ref,
    nf_ref,
    kv,
):
    fill_keys(kv, own_ref, beside_ref, mine_ref, other_ref)
    allowed = (key_ref[0:1, :] <= row_ref[:, 0:1]) & (key_ref[1:2, :] == row_ref[:, 1:2])
    lane = lanes()
    stats = jnp.zeros((ROWS, TILE), F32)
    for j in range(4):
        keys = kv[:, j * 128 : (j + 1) * 128]
        vals = kv[:, 512 + j * 128 : 512 + (j + 1) * 128]
        parts = []
        for h in range(4):
            scores = mm(q_ref[j, h * ROWS : (h + 1) * ROWS, :], keys, NT)
            scores = jnp.where(allowed, scores, -1e30)
            top = jnp.max(scores, axis=1, keepdims=True)
            powers = jnp.exp(scores - top)
            total = jnp.sum(powers, axis=1, keepdims=True)
            stats = jnp.where(lane == 4 * j + h, top + jnp.log(total), stats)
            probs = (powers * (1.0 / total)).astype(BF)
            parts.append(mm(probs, vals))
        low, high = merge_heads(parts, lane)
        heads_ref[:, j * 256 : j * 256 + 128] = low.astype(BF)
        heads_ref[:, j * 256 + 128 : j * 256 + 256] = high.astype(BF)
    lse_ref[...] = stats.T
    middle = tok_ref[...].astype(F32) + mm(heads_ref[...], w_out_ref[...])
    mid_ref[...] = middle
    nf_ref[...] = (middle * rms_parts(middle) * gain_ref[...]).astype(BF)


def middle_kernel(
    backs,
    nf_ref,
    mid_ref,
    gout_ref,
    gain_ref,
    routes_ref,
    router_ref,
    w_out_ref,
    gmid_ref,
    rest_ref,
    g_pad,
    cols_ref,
):
    lane = lanes()
    total = jnp.zeros((ROWS, D), F32)
    grad_gates = jnp.zeros((ROWS, TILE), F32)
    for r in range(8):
        total = total + backs[r, :, 0:D].astype(F32)
        tail = backs[r, :, D:WIDE].astype(F32)
        tail = jnp.where(lane < 4, tail + pltpu.roll(tail, TILE - 4, 1), 0.0)
        grad_gates = grad_gates + (pltpu.roll(tail, 4 * r, 1) if r else tail)
    chosen = lane < 0
    for k in range(8):
        chosen = chosen | (lane == routes_ref[:, k : k + 1])
    logits = mm(nf_ref[...], router_ref[...])
    top = jnp.max(jnp.where(chosen, logits, -3e38), axis=1, keepdims=True)
    powers = jnp.where(chosen, jnp.exp(jnp.minimum(logits - top, 0.0)), 0.0)
    gates = powers / jnp.sum(powers, axis=1, keepdims=True)
    mean = jnp.sum(gates * grad_gates, axis=1, keepdims=True)
    grad_logits = (gates * (grad_gates - mean)).astype(BF)
    total = total + mm(grad_logits, router_ref[...], NT)
    middle = mid_ref[...]
    scale = rms_parts(middle)
    gain_column = column_sums(total * middle * scale)
    router_part = mm(nf_ref[...], grad_logits, TN)
    rest_ref[...] = jnp.where(lanes(D) == 33, gain_column, router_part)
    grad_middle = gout_ref[...].astype(F32) + rms_back(middle, scale, gain_ref[...], total)
    gmid_ref[...] = grad_middle
    branch = grad_middle.astype(BF)
    for t in range(8):
        cols_ref[t] = branch[:, t * TILE : (t + 1) * TILE]
        tile = mm(branch, w_out_ref[t * TILE : (t + 1) * TILE, :], NT)
        put_padded(g_pad, t, tile, lane)


def back_kernel(
    g_pad,
    q_ref,
    own_ref,
    beside_ref,
    mine_ref,
    other_ref,
    lse_ref,
    row_ref,
    key_ref,
    cos_ref,
    sin_ref,
    branch_ref,
    after_0_ref,
    after_1_ref,
    after_2_ref,
    cols_ref,
    gq_ref,
    dkv_mine_ref,
    dkv_other_ref,
    kv,
):
    fill_keys(kv, own_ref, beside_ref, mine_ref, other_ref)
    lane = lanes()
    allowed = (key_ref[:, 0:1] <= row_ref[0:1, :]) & (key_ref[:, 1:2] == row_ref[1:2, :])
    cosine, sine = cos_ref[...], sin_ref[...]
    for j in range(4):
        keys = kv[:, j * 128 : (j + 1) * 128]
        vals = kv[:, 512 + j * 128 : 512 + (j + 1) * 128]
        parts = []
        grad_keys = jnp.zeros((8 * ROWS, 128), F32)
        grad_vals = jnp.zeros((8 * ROWS, 128), F32)
        for h in range(4):
            query = q_ref[j, h * ROWS : (h + 1) * ROWS, :]
            grads = g_pad[j, h * ROWS : (h + 1) * ROWS, :]
            scores = jnp.where(allowed, mm(keys, query, NT), -1e30)
            probs = jnp.exp(scores - lse_ref[4 * j + h : 4 * j + h + 1, :])
            grad_probs = mm(vals, grads, NT)
            delta = jnp.sum(probs * grad_probs, axis=0, keepdims=True)
            grad_scores = (probs * (grad_probs - delta)).astype(BF)
            grad_keys = grad_keys + mm(grad_scores, query)
            grad_vals = grad_vals + mm(probs.astype(BF), grads)
            parts.append(mm(grad_scores, keys, TN))
        for g, tile in enumerate(merge_heads(parts, lane)):
            tile = tile * (HD**-0.5)
            tile = (tile * cosine - partner(tile, lane) * sine).astype(BF)
            t = 2 * j + g
            cols_ref[t, :, 0:TILE] = branch_ref[t]
            cols_ref[t, :, TILE : 2 * TILE] = tile
            gq_ref[:, t * TILE : (t + 1) * TILE] = tile
        for ref, at in ((dkv_mine_ref, 0), (dkv_other_ref, 4)):
            for k in range(4):
                rows = slice((at + k) * ROWS, (at + k + 1) * ROWS)
                ref[k, :, j * 128 : (j + 1) * 128] = grad_keys[rows].astype(BF)
                ref[k, :, 512 + j * 128 : 512 + (j + 1) * 128] = grad_vals[rows].astype(BF)


def turn_kernel(own_ref, a_ref, b_ref, c_ref, cos_ref, sin_ref, early_ref, *refs):
    cols_ref = refs[-1]
    lane = lanes()
    for t in range(8):
        at = slice(t * TILE, (t + 1) * TILE)
        tile = own_ref[:, at] + a_ref[:, at].astype(F32)
        tile = tile + b_ref[:, at].astype(F32) + c_ref[:, at].astype(F32)
        if t < 4:
            tile = tile * cos_ref[...] - partner(tile, lane) * sin_ref[...]
        cols_ref[t, :, 0 : 2 * TILE] = early_ref[t]
        cols_ref[t, :, 2 * TILE : 3 * TILE] = tile.astype(BF)


def last_kernel(gq_ref, cols_ref, w_ref, tok_ref, gain_ref, gmid_ref, rest_ref, *refs):
    gtok_ref, side_ref = refs[-2:]
    grad = mm(gq_ref[...], w_ref[:, 0:D], NT)
    for t in range(8):
        grad = grad + mm(cols_ref[t, :, 2 * TILE : 3 * TILE], w_ref[:, D + t * TILE : D + (t + 1) * TILE], NT)
    values = tok_ref[...].astype(F32)
    scale = rms_parts(values)
    column = column_sums(grad * values * scale)
    side_ref[...] = jnp.where(lanes(D) == 32, column, rest_ref[...]).astype(BF)
    grad_values = gmid_ref[...] + rms_back(values, scale, gain_ref[...], grad)
    gtok_ref[...] = grad_values.astype(BF)


def experts_kernel(order_ref, *refs):
    blocks, refs = refs[:8], refs[8:]
    told_ref, router_ref, wg_ref, wu_ref, wd_ref, made_ref, back_ref, keep_ref, give_ref = refs[:9]
    xs, gs, sel, gate_rows, gg, grad_ref = refs[9:]
    e = pl.program_id(0)
    count = 8 * CAP

    @pl.when(e == 0)
    def _():
        upper = (
            lax.broadcasted_iota(jnp.int32, (ROWS, ROWS), 0)
            <= lax.broadcasted_iota(jnp.int32, (ROWS, ROWS), 1)
        ).astype(BF)
        names = (lax.broadcasted_iota(jnp.int32, (32, ROWS), 0) + 4 * order_ref[8]) % 32
        slots = lax.broadcasted_iota(jnp.int32, (CAP, ROWS), 0)
        for b in range(8):
            told = told_ref[order_ref[b]]
            routes = told[:, D:WIDE].astype(F32).T[0:8].astype(jnp.int32)
            chosen = jnp.zeros((32, ROWS), F32)
            for k in range(8):
                chosen = jnp.where(names == routes[k : k + 1, :], 1.0, chosen)
            place = mm(chosen.astype(BF), upper).astype(jnp.int32) - 1
            logits = mm(router_ref[...], blocks[b][...], NT)
            top = jnp.max(jnp.where(chosen > 0, logits, -3e38), axis=0, keepdims=True)
            powers = jnp.where(chosen > 0, jnp.exp(jnp.minimum(logits - top, 0.0)), 0.0)
            weights = powers / jnp.sum(powers, axis=0, keepdims=True)
            for c in range(4):
                hit = (slots == place[c : c + 1, :]) & (chosen[c : c + 1, :] > 0)
                sel[b, c * CAP : (c + 1) * CAP, :] = hit.astype(F32).astype(BF)
                gate_rows[c, b] = jnp.sum(
                    jnp.where(hit, weights[c : c + 1, :], 0.0), axis=1, keepdims=True
                )
            xs[b] = mm(sel[b], blocks[b][...]).astype(BF)
            gs[b] = mm(sel[b], told[:, 0:D]).astype(BF)
            gg[b] = jnp.zeros((8, ROWS), F32)

    at = pl.ds(pl.multiple_of(e * CAP, CAP), CAP)
    rows = xs[:, at, :].reshape(count, D)
    grads = gs[:, at, :].reshape(count, D).astype(F32)
    weight = gate_rows[e].reshape(count, 1)
    gate_act = mm(rows, wg_ref[0])
    up_act = mm(rows, wu_ref[0])
    sig = 1.0 / (1.0 + jnp.exp(-gate_act))
    silu = gate_act * sig
    hidden = (silu * up_act).astype(BF)
    made = mm(hidden, wd_ref[0])
    grad_gate = jnp.sum(made * grads, axis=1, keepdims=True).reshape(8, CAP, 1)
    grad_rows = (weight * grads).astype(BF)
    grad_hidden = mm(grad_rows, wd_ref[0], NT)
    grad_gate_act = (grad_hidden * up_act * (sig * (1.0 + gate_act * (1.0 - sig)))).astype(BF)
    grad_up_act = (grad_hidden * silu).astype(BF)
    grad_ref[:, 64:96, :] = mm(hidden, grad_rows, TN).astype(BF).reshape(16, 32, D)
    joint = mm(rows, jnp.concatenate([grad_gate_act, grad_up_act], axis=1), TN)
    grad_ref[:, 0:64, :] = joint.astype(BF).reshape(16, 64, D)
    for c, ref in enumerate((keep_ref, give_ref)):
        for d in range(2):
            for z in range(4):
                ring = (order_ref[10] + z) % 4
                ref[d, z, 0] = grad_ref[(order_ref[9] ^ d) * 8 + ring * 2 + (order_ref[11] ^ c)]
    xs[:, at, :] = (weight * made).astype(BF).reshape(8, CAP, D)
    grad_x = mm(grad_gate_act, wg_ref[0], NT) + mm(grad_up_act, wu_ref[0], NT)
    gs[:, at, :] = grad_x.astype(BF).reshape(8, CAP, D)
    sub = lax.broadcasted_iota(jnp.int32, (8, ROWS), 0)
    for b in range(8):
        line = jnp.sum(sel[b, at, :].astype(F32) * grad_gate[b], axis=0, keepdims=True)
        high = line.astype(BF).astype(F32)
        gg[b] = jnp.where(sub == e, high, jnp.where(sub == e + 4, line - high, gg[b]))

    @pl.when(e == 3)
    def _():
        for b in range(8):
            to = order_ref[b]
            made_ref[to] = mm(sel[b], xs[b], TN).astype(BF)
            back_ref[to, :, 0:D] = mm(sel[b], gs[b], TN).astype(BF)
            tall = jnp.concatenate([gg[b], jnp.zeros((ROWS - 8, ROWS), F32)], axis=0)
            back_ref[to, :, D:WIDE] = tall.T.astype(BF)


def experts(order, blocks, told, router_rel, w_gate, w_up, w_down):
    whole = lambda *shape: pl.BlockSpec(shape, lambda e, order: (0,) * len(shape))
    return pl.pallas_call(
        experts_kernel,
        grid_spec=pltpu.PrefetchScalarGridSpec(
            num_scalar_prefetch=1,
            grid=(4,),
            in_specs=[whole(ROWS, D)] * 8
            + [
                whole(8, ROWS, WIDE),
                whole(32, D),
                pl.BlockSpec((1, D, FF), lambda e, order: (e, 0, 0)),
                pl.BlockSpec((1, D, FF), lambda e, order: (e, 0, 0)),
                pl.BlockSpec((1, FF, D), lambda e, order: (e, 0, 0)),
            ],
            out_specs=[
                whole(8, ROWS, D),
                whole(8, ROWS, WIDE),
                pl.BlockSpec((2, 4, 1, 96, D), lambda e, order: (0, 0, e, 0, 0)),
                pl.BlockSpec((2, 4, 1, 96, D), lambda e, order: (0, 0, e, 0, 0)),
            ],
            scratch_shapes=[
                pltpu.VMEM((8, 4 * CAP, D), BF),
                pltpu.VMEM((8, 4 * CAP, D), BF),
                pltpu.VMEM((8, 4 * CAP, ROWS), BF),
                pltpu.VMEM((4, 8, CAP, 1), F32),
                pltpu.VMEM((8, 8, ROWS), F32),
                pltpu.VMEM((16, 96, D), BF),
            ],
        ),
        out_shape=[
            shaped(BF, 8, ROWS, D),
            shaped(BF, 8, ROWS, WIDE),
            shaped(BF, 2, 4, 4, 96, D),
            shaped(BF, 2, 4, 4, 96, D),
        ],
        compiler_params=pltpu.CompilerParams(
            dimension_semantics=("arbitrary",), vmem_limit_bytes=VMEM_BYTES
        ),
        name="experts",
    )(order, *blocks, told, router_rel, w_gate, w_up, w_down)


ANY = pl.BlockSpec(memory_space=pl.ANY)


def hold_kernel(value_ref, after_ref, out_ref):
    out_ref[...] = value_ref[...]


def join_x_kernel(keep_ref, got_ref, *refs):
    for d in range(2):
        both = keep_ref[d, 0].astype(F32) + got_ref[d, 0].astype(F32)
        refs[d - 2][0] = both.astype(BF)


def join_x(keep, got, start, after):
    block = pl.BlockSpec((2, 1, 2, 96, D), lambda z: (0, z, start // 2, 0, 0))
    return kernel_call(
        join_x_kernel,
        "join_x",
        [shaped(BF, 4, 2, 96, D)] * 2,
        grid=(4,),
        in_specs=[block, block] + [ANY] * len(after),
        out_specs=[pl.BlockSpec((1, 2, 96, D), lambda z: (z, 0, 0, 0))] * 2,
    )(keep, got, *after)


def join_rings_kernel(keep_ref, got_ref, *refs):
    for z in range(4):
        both = keep_ref[0, z, 0].astype(F32) + got_ref[0, z, 0].astype(F32)
        refs[z - 4][0, 0] = both.astype(BF)


def sum_z_first(keep, got, start):
    block = pl.BlockSpec((1, 4, 1, 96, D), lambda d, e: (d, 0, start + e, 0, 0))
    here, ahead, across, behind = kernel_call(
        join_rings_kernel,
        "join_rings",
        [shaped(BF, 2, 2, 96, D)] * 4,
        grid=(2, 2),
        in_specs=[block, block],
        out_specs=[pl.BlockSpec((1, 1, 96, D), lambda d, e: (d, e, 0, 0))] * 4,
    )(keep, got)
    came = [send(ahead, "ctx", up), send(behind, "ctx", down), send(across, "ctx", far)]
    half = lambda d: here[d].astype(F32) + sum(v[d].astype(F32) for v in came)
    return half(0) + send(half(1).astype(BF), "dp", beside).astype(F32), came, here


def join_z_kernel(own_ref, got_ref, *refs):
    for z in range(4):
        refs[z - 4][0] = (own_ref[z, 0].astype(F32) + got_ref[z, 0].astype(F32)).astype(BF)


def sum_z(own, got, after):
    block = pl.BlockSpec((4, 1, 96, D), lambda e: (0, e, 0, 0))
    here, ahead, across, behind = kernel_call(
        join_z_kernel,
        "join_z",
        [shaped(BF, 2, 96, D)] * 4,
        grid=(2,),
        in_specs=[block, block] + [ANY] * len(after),
        out_specs=[pl.BlockSpec((1, 96, D), lambda e: (e, 0, 0))] * 4,
    )(own, got, *after)
    came = [send(ahead, "ctx", up), send(behind, "ctx", down), send(across, "ctx", far)]
    return here.astype(F32) + sum(v.astype(F32) for v in came), came, here


def join_kv_kernel(mine_ref, got_ref, *refs):
    own, outs = refs[-4], refs[-3:]
    own[...] = mine_ref[0].astype(F32) + got_ref[0].astype(F32)
    for k in range(3):
        outs[k][...] = (mine_ref[k + 1].astype(F32) + got_ref[k + 1].astype(F32)).astype(BF)


def to_all(value, axis):
    return lax.all_to_all(value, axis, 0, 0, tiled=True)


def local(
    tokens,
    doc_ids,
    gain_attn,
    w_qkv,
    w_out,
    gain_ffn,
    w_router,
    routes,
    w_gate,
    w_up,
    w_down,
    grad_output,
):
    vmem = pl.BlockSpec(memory_space=pltpu.VMEM)
    ctx = lax.axis_index("ctx")
    me = lax.axis_index("expert")
    gain_first = gain_attn.astype(F32)[None, :]
    gain_second = gain_ffn.astype(F32)[None, :]

    named = jnp.pad(routes[0].astype(BF), ((0, 0), (0, TILE - 8)))
    told = jnp.concatenate([grad_output[0], named], axis=1)
    told = lax.all_gather(told, "expert", axis=0)

    places = ctx * ROWS + jnp.arange(ROWS, dtype=jnp.int32)
    lane = jnp.arange(TILE)
    frequency = 10000.0 ** (-(lane % 32).astype(F32) / (HD // 2))
    angles = places.astype(F32)[:, None] * frequency[None, :]
    cosine = jnp.cos(angles)
    sine = jnp.sin(angles) * jnp.where(lane % HD < HD // 2, -1.0, 1.0)[None, :]
    normed, q_pad, kv_own = kernel_call(
        first_kernel,
        "project",
        (shaped(BF, ROWS, D), shaped(BF, 4, 4 * ROWS, TILE), shaped(BF, ROWS, D)),
    )(tokens[0], gain_first, w_qkv, cosine, sine)

    normed_all = lax.all_gather(normed, "expert", axis=0, tiled=True)
    kv_mine = [send(kv_own, "ctx", to) for to in (down, up, far)]
    kv_beside = send(kv_own, "ctx", beside)
    kv_mine = jnp.stack(kv_mine)
    kv_other = send(kv_mine, "ctx", beside)
    keys = (kv_own, kv_beside, kv_mine, kv_other)

    docs = doc_ids[0].reshape(8, ROWS)
    ring = jnp.array([0, 2, -2, 4], jnp.int32)
    block_ids = jnp.concatenate([ctx + ring, jnp.bitwise_xor(ctx, 1) + ring]) % 8
    picks = (block_ids[:, None] == jnp.arange(8)[None, :]).astype(jnp.int32)
    key_docs = jnp.sum(picks[:, :, None] * docs[None], axis=1).reshape(-1)
    key_places = (block_ids[:, None] * ROWS + jnp.arange(ROWS)[None, :]).reshape(-1)
    own_docs = jnp.sum((jnp.arange(8) == ctx).astype(jnp.int32)[:, None] * docs, axis=0)
    row_info = jnp.stack([places, own_docs])
    key_info = jnp.stack([key_places, key_docs]).astype(jnp.int32)

    heads, lse, middle, normed_ffn = kernel_call(
        attend_kernel,
        "attend",
        (
            shaped(BF, ROWS, D),
            shaped(F32, ROWS, TILE),
            shaped(F32, ROWS, D),
            shaped(BF, ROWS, D),
        ),
        scratch_shapes=[pltpu.VMEM((8 * ROWS, D), BF)],
    )(q_pad, *keys, row_info.T, key_info, w_out, tokens[0], gain_second)

    heads_all = lax.all_gather(heads, "expert", axis=0, tiled=True)

    from_up, from_down, from_far = (send(normed_ffn, "expert", to) for to in (down, up, far))
    from_beside = send(normed_ffn, "expert", beside)
    other_up, other_down = (send(from_beside, "expert", to) for to in (down, up))
    other_far = send(from_far, "expert", beside)
    router_rel = jnp.roll(w_router, -4 * me, axis=1).T
    pair = jnp.bitwise_xor(me, 1)
    order = [me, pair, up(me), (me + 6) % 8, far(me), up(pair), (pair + 6) % 8, far(pair), me]
    order += [lax.axis_index("dp"), ctx // 2, ctx % 2]
    blocks = (normed_ffn, from_beside, from_up, from_down)
    blocks += (from_far, other_up, other_down, other_far)
    made, back, keep, give = experts(
        jnp.stack(order).astype(jnp.int32), blocks, told, router_rel, w_gate, w_up, w_down
    )
    back = to_all(back, "expert")
    given = send(give, "ctx", beside)
    own_0, other_0 = join_x(keep, given, 0, [])
    crossed_0 = send(other_0, "dp", beside)
    sums_1, came_1, own_1 = sum_z_first(keep, given, 2)
    made = kernel_call(hold_kernel, "hold", shaped(BF, 8, ROWS, D), in_specs=[vmem, ANY])(made, back)
    made = to_all(made, "expert")

    router_wide = jnp.pad(w_router, ((0, 0), (0, TILE - 32)))
    operands = (
        back,
        normed_ffn,
        middle,
        grad_output[0],
        gain_second,
        routes[0],
        router_wide,
        w_out,
    )
    grad_middle, rest, g_pad, branch = kernel_call(
        middle_kernel,
        "middle_back",
        (
            shaped(F32, ROWS, D),
            shaped(F32, D, TILE),
            shaped(BF, 4, 4 * ROWS, TILE),
            shaped(BF, 8, ROWS, TILE),
        ),
        in_specs=[vmem] * len(operands),
    )(*operands)
    cols, grad_q, dkv_mine, dkv_other = kernel_call(
        back_kernel,
        "attend_back",
        (
            shaped(BF, 8, ROWS, 2 * TILE),
            shaped(BF, ROWS, D),
            shaped(BF, 4, ROWS, D),
            shaped(BF, 4, ROWS, D),
        ),
        in_specs=[vmem] * 12 + [ANY] * 3,
        scratch_shapes=[pltpu.VMEM((8 * ROWS, D), BF)],
    )(g_pad, q_pad, *keys, lse, row_info, key_info.T, cosine, sine, branch, *came_1)

    own, *parts = kernel_call(
        join_kv_kernel,
        "join_kv",
        [shaped(F32, ROWS, D)] + [shaped(BF, ROWS, D)] * 3,
        in_specs=[vmem] * 2 + [ANY],
    )(dkv_mine, send(dkv_other, "ctx", beside), crossed_0)
    arrived = [send(v, "ctx", to) for v, to in zip(parts, (up, down, far))]
    sums_0, came_0, here_0 = sum_z(own_0, crossed_0, [own])
    cols = kernel_call(
        turn_kernel, "turn", shaped(BF, 8, ROWS, 3 * TILE), in_specs=[vmem] * 7 + [ANY] * 2
    )(own, *arrived, cosine, sine, cols, made, here_0)
    here = to_all(cols, "expert")
    here = here.reshape(8 * ROWS, 3 * TILE)
    grad_tokens, side = kernel_call(
        last_kernel,
        "grad_tokens",
        (shaped(BF, ROWS, D), shaped(BF, D, TILE)),
        in_specs=[vmem] * 7 + [ANY] * 3,
    )(grad_q, cols, w_qkv, tokens[0], gain_first, grad_middle, rest, *came_0)
    output = (middle + jnp.sum(made.astype(F32), axis=0)).astype(BF)

    out_cols = mm(heads_all, here[:, :TILE], TN).astype(BF)
    mixed_cols = mm(normed_all, here[:, TILE:], TN).astype(BF)
    dense = jnp.concatenate([mixed_cols, out_cols, side], axis=1)
    dense = jnp.sum(to_all(dense.reshape(16, 64, 4 * TILE), ("dp", "ctx")).astype(F32), axis=0)
    dense = to_all(dense.astype(BF).reshape(8, 8, 4 * TILE), "expert").astype(F32)
    tiles = jnp.transpose(dense[:, :, : 3 * TILE].reshape(8, 8, 3, TILE), (1, 2, 0, 3))
    rest = jnp.sum(dense[:, :, 3 * TILE :], axis=0)
    parts = jnp.concatenate([sums_0, sums_1], axis=0)
    return (
        output[None],
        grad_tokens[None],
        rest[:, 32],
        tiles[:, :2].reshape(8, 2 * D),
        tiles[:, 2].reshape(8, D),
        rest[:, 33],
        rest[:, :32],
        parts[:, :64, :FF],
        parts[:, :64, FF:],
        parts[:, 64:, :],
    )


def solution(mesh):
    in_specs = (
        P(("dp", "expert"), "ctx", None),
        P(("dp", "expert"), None),
        P(),
        P(),
        P(),
        P(),
        P(),
        P(("dp", "expert"), "ctx", None),
        P("expert", None, None),
        P("expert", None, None),
        P("expert", None, None),
        P(("dp", "expert"), "ctx", None),
    )
    out_specs = (
        P(("dp", "expert"), "ctx", None),
        P(("dp", "expert"), "ctx", None),
        P(("dp", "ctx", "expert")),
        P(("dp", "ctx", "expert"), None),
        P(("dp", "ctx", "expert"), None),
        P(("dp", "ctx", "expert")),
        P(("dp", "ctx", "expert"), None),
        P("expert", ("dp", "ctx"), None),
        P("expert", ("dp", "ctx"), None),
        P("expert", ("dp", "ctx"), None),
    )
    return jax.shard_map(local, mesh=mesh, in_specs=in_specs, out_specs=out_specs, check_vma=False)
```

```python
import functools

import jax
import jax.numpy as jnp
from jax import lax
from jax.experimental import pallas as pl
from jax.experimental.pallas import tpu as pltpu
from jax.sharding import PartitionSpec as P

D = 1024
FF = 512
QH = 16
KVH = 8
HD = 64
ROWS = 128
CAP = 64
TILE = 128
WIDE = D + TILE
BF = jnp.bfloat16
F32 = jnp.float32
VMEM_BYTES = 60 * 1024 * 1024

NN = (((1,), (0,)), ((), ()))
NT = (((1,), (1,)), ((), ()))
TN = (((0,), (0,)), ((), ()))


def mm(a, b, dims=NN):
    return lax.dot_general(a, b, dims, preferred_element_type=F32)


def send(value, axis, to):
    return lax.ppermute(value, axis, [(i, to(i)) for i in range(lax.axis_size(axis))])


def up(i):
    return (i + 2) % 8


def down(i):
    return (i - 2) % 8


def far(i):
    return (i + 4) % 8


def beside(i):
    return i ^ 1


def kernel_call(body, name, out_shape, **more):
    return pl.pallas_call(
        body,
        out_shape=out_shape,
        compiler_params=pltpu.CompilerParams(vmem_limit_bytes=VMEM_BYTES),
        name=name,
        **more,
    )


def shaped(dtype, *shape):
    return jax.ShapeDtypeStruct(shape, dtype)


def lanes(rows=ROWS):
    return lax.broadcasted_iota(jnp.int32, (rows, TILE), 1)


def rms_parts(values):
    return lax.rsqrt(jnp.mean(values * values, axis=-1, keepdims=True) + 1e-06)


def rms_back(values, scale, gain, grad):
    weighted = grad * gain
    inner = jnp.mean(values * weighted, axis=-1, keepdims=True)
    return scale * weighted - values * (scale * scale * scale) * inner


def partner(tile, lane):
    return jnp.where(lane % HD < HD // 2, pltpu.roll(tile, TILE - 32, 1), pltpu.roll(tile, 32, 1))


def put_padded(ref, t, tile, lane):
    turned = pltpu.roll(tile, HD, 1)
    j, g = t // 2, t % 2
    own = (lane < HD) if g == 0 else (lane >= HD)
    first, second = (tile, turned) if g == 0 else (turned, tile)
    at = 2 * g * ROWS
    ref[j, at : at + ROWS, :] = jnp.where(own, first, 0.0).astype(BF)
    ref[j, at + ROWS : at + 2 * ROWS, :] = jnp.where(own, second, 0.0).astype(BF)


def merge_heads(parts, lane):
    low = jnp.where(lane < HD, parts[0], pltpu.roll(parts[1], HD, 1))
    high = jnp.where(lane < HD, pltpu.roll(parts[2], HD, 1), parts[3])
    return low, high


def column_sums(values):
    high = values.astype(BF)
    low = (values - high.astype(F32)).astype(BF)
    ones = jnp.ones((ROWS, TILE), BF)
    return mm(high, ones, TN) + mm(low, ones, TN)


def first_kernel(tok_ref, gain_ref, w_ref, cos_ref, sin_ref, normed_ref, q_ref, kv_ref):
    values = tok_ref[...].astype(F32)
    normed = (values * rms_parts(values) * gain_ref[...]).astype(BF)
    normed_ref[...] = normed
    lane = lanes()
    cosine, sine = cos_ref[...], sin_ref[...]
    for t in range(16):
        tile = mm(normed, w_ref[:, t * TILE : (t + 1) * TILE])
        if t < 12:
            tile = tile * cosine + partner(tile, lane) * sine
        if t < 8:
            put_padded(q_ref, t, tile.astype(BF).astype(F32) * (HD**-0.5), lane)
        else:
            kv_ref[:, (t - 8) * TILE : (t - 7) * TILE] = tile.astype(BF)


def fill_keys(kv, own_ref, beside_ref, mine_ref, other_ref):
    kv[0:ROWS] = own_ref[...]
    kv[4 * ROWS : 5 * ROWS] = beside_ref[...]
    for k in range(3):
        kv[(k + 1) * ROWS : (k + 2) * ROWS] = mine_ref[k]
        kv[(k + 5) * ROWS : (k + 6) * ROWS] = other_ref[k]


def attend_kernel(
    q_ref,
    own_ref,
    beside_ref,
    mine_ref,
    other_ref,
    row_ref,
    key_ref,
    w_out_ref,
    tok_ref,
    gain_ref,
    heads_ref,
    lse_ref,
    mid_ref,
    nf_ref,
    kv,
):
    fill_keys(kv, own_ref, beside_ref, mine_ref, other_ref)
    allowed = (key_ref[0:1, :] <= row_ref[:, 0:1]) & (key_ref[1:2, :] == row_ref[:, 1:2])
    lane = lanes()
    stats = jnp.zeros((ROWS, TILE), F32)
    for j in range(4):
        keys = kv[:, j * 128 : (j + 1) * 128]
        vals = kv[:, 512 + j * 128 : 512 + (j + 1) * 128]
        parts = []
        for h in range(4):
            scores = mm(q_ref[j, h * ROWS : (h + 1) * ROWS, :], keys, NT)
            scores = jnp.where(allowed, scores, -1e30)
            top = jnp.max(scores, axis=1, keepdims=True)
            powers = jnp.exp(scores - top)
            total = jnp.sum(powers, axis=1, keepdims=True)
            stats = jnp.where(lane == 4 * j + h, top + jnp.log(total), stats)
            probs = (powers * (1.0 / total)).astype(BF)
            parts.append(mm(probs, vals))
        low, high = merge_heads(parts, lane)
        heads_ref[:, j * 256 : j * 256 + 128] = low.astype(BF)
        heads_ref[:, j * 256 + 128 : j * 256 + 256] = high.astype(BF)
    lse_ref[...] = stats.T
    middle = tok_ref[...].astype(F32) + mm(heads_ref[...], w_out_ref[...])
    mid_ref[...] = middle
    nf_ref[...] = (middle * rms_parts(middle) * gain_ref[...]).astype(BF)


def middle_kernel(
    backs,
    nf_ref,
    mid_ref,
    gout_ref,
    gain_ref,
    routes_ref,
    router_ref,
    w_out_ref,
    gmid_ref,
    rest_ref,
    g_pad,
    cols_ref,
):
    lane = lanes()
    total = jnp.zeros((ROWS, D), F32)
    grad_gates = jnp.zeros((ROWS, TILE), F32)
    for r in range(8):
        total = total + backs[r, :, 0:D].astype(F32)
        tail = backs[r, :, D:WIDE].astype(F32)
        tail = jnp.where(lane < 4, tail + pltpu.roll(tail, TILE - 4, 1), 0.0)
        grad_gates = grad_gates + (pltpu.roll(tail, 4 * r, 1) if r else tail)
    chosen = lane < 0
    for k in range(8):
        chosen = chosen | (lane == routes_ref[:, k : k + 1])
    logits = mm(nf_ref[...], router_ref[...])
    top = jnp.max(jnp.where(chosen, logits, -3e38), axis=1, keepdims=True)
    powers = jnp.where(chosen, jnp.exp(jnp.minimum(logits - top, 0.0)), 0.0)
    gates = powers / jnp.sum(powers, axis=1, keepdims=True)
    mean = jnp.sum(gates * grad_gates, axis=1, keepdims=True)
    grad_logits = (gates * (grad_gates - mean)).astype(BF)
    total = total + mm(grad_logits, router_ref[...], NT)
    middle = mid_ref[...]
    scale = rms_parts(middle)
    gain_column = column_sums(total * middle * scale)
    router_part = mm(nf_ref[...], grad_logits, TN)
    rest_ref[...] = jnp.where(lanes(D) == 33, gain_column, router_part)
    grad_middle = gout_ref[...].astype(F32) + rms_back(middle, scale, gain_ref[...], total)
    gmid_ref[...] = grad_middle
    branch = grad_middle.astype(BF)
    for t in range(8):
        cols_ref[t] = branch[:, t * TILE : (t + 1) * TILE]
        tile = mm(branch, w_out_ref[t * TILE : (t + 1) * TILE, :], NT)
        put_padded(g_pad, t, tile, lane)


def back_kernel(
    g_pad,
    q_ref,
    own_ref,
    beside_ref,
    mine_ref,
    other_ref,
    lse_ref,
    row_ref,
    key_ref,
    cos_ref,
    sin_ref,
    branch_ref,
    after_0_ref,
    after_1_ref,
    after_2_ref,
    cols_ref,
    gq_ref,
    dkv_mine_ref,
    dkv_other_ref,
    kv,
):
    fill_keys(kv, own_ref, beside_ref, mine_ref, other_ref)
    lane = lanes()
    allowed = (key_ref[:, 0:1] <= row_ref[0:1, :]) & (key_ref[:, 1:2] == row_ref[1:2, :])
    cosine, sine = cos_ref[...], sin_ref[...]
    for j in range(4):
        keys = kv[:, j * 128 : (j + 1) * 128]
        vals = kv[:, 512 + j * 128 : 512 + (j + 1) * 128]
        parts = []
        grad_keys = jnp.zeros((8 * ROWS, 128), F32)
        grad_vals = jnp.zeros((8 * ROWS, 128), F32)
        for h in range(4):
            query = q_ref[j, h * ROWS : (h + 1) * ROWS, :]
            grads = g_pad[j, h * ROWS : (h + 1) * ROWS, :]
            scores = jnp.where(allowed, mm(keys, query, NT), -1e30)
            probs = jnp.exp(scores - lse_ref[4 * j + h : 4 * j + h + 1, :])
            grad_probs = mm(vals, grads, NT)
            delta = jnp.sum(probs * grad_probs, axis=0, keepdims=True)
            grad_scores = (probs * (grad_probs - delta)).astype(BF)
            grad_keys = grad_keys + mm(grad_scores, query)
            grad_vals = grad_vals + mm(probs.astype(BF), grads)
            parts.append(mm(grad_scores, keys, TN))
        for g, tile in enumerate(merge_heads(parts, lane)):
            tile = tile * (HD**-0.5)
            tile = (tile * cosine - partner(tile, lane) * sine).astype(BF)
            t = 2 * j + g
            cols_ref[t, :, 0:TILE] = branch_ref[t]
            cols_ref[t, :, TILE : 2 * TILE] = tile
            gq_ref[:, t * TILE : (t + 1) * TILE] = tile
        for ref, at in ((dkv_mine_ref, 0), (dkv_other_ref, 4)):
            for k in range(4):
                rows = slice((at + k) * ROWS, (at + k + 1) * ROWS)
                ref[k, :, j * 128 : (j + 1) * 128] = grad_keys[rows].astype(BF)
                ref[k, :, 512 + j * 128 : 512 + (j + 1) * 128] = grad_vals[rows].astype(BF)


def turn_kernel(own_ref, a_ref, b_ref, c_ref, cos_ref, sin_ref, early_ref, *refs):
    cols_ref = refs[-1]
    lane = lanes()
    for t in range(8):
        at = slice(t * TILE, (t + 1) * TILE)
        tile = own_ref[:, at] + a_ref[:, at].astype(F32)
        tile = tile + b_ref[:, at].astype(F32) + c_ref[:, at].astype(F32)
        if t < 4:
            tile = tile * cos_ref[...] - partner(tile, lane) * sin_ref[...]
        cols_ref[t, :, 0 : 2 * TILE] = early_ref[t]
        cols_ref[t, :, 2 * TILE : 3 * TILE] = tile.astype(BF)


def last_kernel(gq_ref, cols_ref, w_ref, tok_ref, gain_ref, gmid_ref, rest_ref, *refs):
    gtok_ref, side_ref = refs[-2:]
    grad = mm(gq_ref[...], w_ref[:, 0:D], NT)
    for t in range(8):
        grad = grad + mm(cols_ref[t, :, 2 * TILE : 3 * TILE], w_ref[:, D + t * TILE : D + (t + 1) * TILE], NT)
    values = tok_ref[...].astype(F32)
    scale = rms_parts(values)
    column = column_sums(grad * values * scale)
    side_ref[...] = jnp.where(lanes(D) == 32, column, rest_ref[...]).astype(BF)
    grad_values = gmid_ref[...] + rms_back(values, scale, gain_ref[...], grad)
    gtok_ref[...] = grad_values.astype(BF)


def experts_kernel(order_ref, *refs):
    blocks, refs = refs[:8], refs[8:]
    told_ref, router_ref, wg_ref, wu_ref, wd_ref, made_ref, back_ref, keep_ref, give_ref = refs[:9]
    xs, gs, sel, gate_rows, gg, grad_ref = refs[9:]
    e = pl.program_id(0)
    count = 8 * CAP

    @pl.when(e == 0)
    def _():
        upper = (
            lax.broadcasted_iota(jnp.int32, (ROWS, ROWS), 0)
            <= lax.broadcasted_iota(jnp.int32, (ROWS, ROWS), 1)
        ).astype(BF)
        names = (lax.broadcasted_iota(jnp.int32, (32, ROWS), 0) + 4 * order_ref[8]) % 32
        slots = lax.broadcasted_iota(jnp.int32, (CAP, ROWS), 0)
        for b in range(8):
            told = told_ref[order_ref[b]]
            routes = told[:, D:WIDE].astype(F32).T[0:8].astype(jnp.int32)
            chosen = jnp.zeros((32, ROWS), F32)
            for k in range(8):
                chosen = jnp.where(names == routes[k : k + 1, :], 1.0, chosen)
            place = mm(chosen.astype(BF), upper).astype(jnp.int32) - 1
            logits = mm(router_ref[...], blocks[b][...], NT)
            top = jnp.max(jnp.where(chosen > 0, logits, -3e38), axis=0, keepdims=True)
            powers = jnp.where(chosen > 0, jnp.exp(jnp.minimum(logits - top, 0.0)), 0.0)
            weights = powers / jnp.sum(powers, axis=0, keepdims=True)
            for c in range(4):
                hit = (slots == place[c : c + 1, :]) & (chosen[c : c + 1, :] > 0)
                sel[b, c * CAP : (c + 1) * CAP, :] = hit.astype(F32).astype(BF)
                gate_rows[c, b] = jnp.sum(
                    jnp.where(hit, weights[c : c + 1, :], 0.0), axis=1, keepdims=True
                )
            xs[b] = mm(sel[b], blocks[b][...]).astype(BF)
            gs[b] = mm(sel[b], told[:, 0:D]).astype(BF)
            gg[b] = jnp.zeros((8, ROWS), F32)

    at = pl.ds(pl.multiple_of(e * CAP, CAP), CAP)
    rows = xs[:, at, :].reshape(count, D)
    grads = gs[:, at, :].reshape(count, D).astype(F32)
    weight = gate_rows[e].reshape(count, 1)
    gate_act = mm(rows, wg_ref[0])
    up_act = mm(rows, wu_ref[0])
    sig = 1.0 / (1.0 + jnp.exp(-gate_act))
    silu = gate_act * sig
    hidden = (silu * up_act).astype(BF)
    made = mm(hidden, wd_ref[0])
    grad_gate = jnp.sum(made * grads, axis=1, keepdims=True).reshape(8, CAP, 1)
    grad_rows = (weight * grads).astype(BF)
    grad_hidden = mm(grad_rows, wd_ref[0], NT)
    grad_gate_act = (grad_hidden * up_act * (sig * (1.0 + gate_act * (1.0 - sig)))).astype(BF)
    grad_up_act = (grad_hidden * silu).astype(BF)
    grad_ref[:, 64:96, :] = mm(hidden, grad_rows, TN).astype(BF).reshape(16, 32, D)
    joint = mm(rows, jnp.concatenate([grad_gate_act, grad_up_act], axis=1), TN)
    grad_ref[:, 0:64, :] = joint.astype(BF).reshape(16, 64, D)
    for c, ref in enumerate((keep_ref, give_ref)):
        for d in range(2):
            for z in range(4):
                ring = (order_ref[10] + z) % 4
                ref[d, z, 0] = grad_ref[(order_ref[9] ^ d) * 8 + ring * 2 + (order_ref[11] ^ c)]
    xs[:, at, :] = (weight * made).astype(BF).reshape(8, CAP, D)
    grad_x = mm(grad_gate_act, wg_ref[0], NT) + mm(grad_up_act, wu_ref[0], NT)
    gs[:, at, :] = grad_x.astype(BF).reshape(8, CAP, D)
    sub = lax.broadcasted_iota(jnp.int32, (8, ROWS), 0)
    for b in range(8):
        line = jnp.sum(sel[b, at, :].astype(F32) * grad_gate[b], axis=0, keepdims=True)
        high = line.astype(BF).astype(F32)
        gg[b] = jnp.where(sub == e, high, jnp.where(sub == e + 4, line - high, gg[b]))

    @pl.when(e == 3)
    def _():
        for b in range(8):
            to = order_ref[b]
            made_ref[to] = mm(sel[b], xs[b], TN).astype(BF)
            back_ref[to, :, 0:D] = mm(sel[b], gs[b], TN).astype(BF)
            tall = jnp.concatenate([gg[b], jnp.zeros((ROWS - 8, ROWS), F32)], axis=0)
            back_ref[to, :, D:WIDE] = tall.T.astype(BF)


def experts(order, blocks, told, router_rel, w_gate, w_up, w_down):
    whole = lambda *shape: pl.BlockSpec(shape, lambda e, order: (0,) * len(shape))
    return pl.pallas_call(
        experts_kernel,
        grid_spec=pltpu.PrefetchScalarGridSpec(
            num_scalar_prefetch=1,
            grid=(4,),
            in_specs=[whole(ROWS, D)] * 8
            + [
                whole(8, ROWS, WIDE),
                whole(32, D),
                pl.BlockSpec((1, D, FF), lambda e, order: (e, 0, 0)),
                pl.BlockSpec((1, D, FF), lambda e, order: (e, 0, 0)),
                pl.BlockSpec((1, FF, D), lambda e, order: (e, 0, 0)),
            ],
            out_specs=[
                whole(8, ROWS, D),
                whole(8, ROWS, WIDE),
                pl.BlockSpec((2, 4, 1, 96, D), lambda e, order: (0, 0, e, 0, 0)),
                pl.BlockSpec((2, 4, 1, 96, D), lambda e, order: (0, 0, e, 0, 0)),
            ],
            scratch_shapes=[
                pltpu.VMEM((8, 4 * CAP, D), BF),
                pltpu.VMEM((8, 4 * CAP, D), BF),
                pltpu.VMEM((8, 4 * CAP, ROWS), BF),
                pltpu.VMEM((4, 8, CAP, 1), F32),
                pltpu.VMEM((8, 8, ROWS), F32),
                pltpu.VMEM((16, 96, D), BF),
            ],
        ),
        out_shape=[
            shaped(BF, 8, ROWS, D),
            shaped(BF, 8, ROWS, WIDE),
            shaped(BF, 2, 4, 4, 96, D),
            shaped(BF, 2, 4, 4, 96, D),
        ],
        compiler_params=pltpu.CompilerParams(
            dimension_semantics=("arbitrary",), vmem_limit_bytes=VMEM_BYTES
        ),
        name="experts",
    )(order, *blocks, told, router_rel, w_gate, w_up, w_down)


ANY = pl.BlockSpec(memory_space=pl.ANY)


def join_x_kernel(keep_ref, got_ref, *refs):
    for d in range(2):
        both = keep_ref[d, 0].astype(F32) + got_ref[d, 0].astype(F32)
        refs[d - 2][0] = both.astype(BF)


def join_x(keep, got, start, after):
    block = pl.BlockSpec((2, 1, 2, 96, D), lambda z: (0, z, start // 2, 0, 0))
    return kernel_call(
        join_x_kernel,
        "join_x",
        [shaped(BF, 4, 2, 96, D)] * 2,
        grid=(4,),
        in_specs=[block, block] + [ANY] * len(after),
        out_specs=[pl.BlockSpec((1, 2, 96, D), lambda z: (z, 0, 0, 0))] * 2,
    )(keep, got, *after)


def join_rings_kernel(keep_ref, got_ref, *refs):
    for z in range(4):
        both = keep_ref[0, z, 0].astype(F32) + got_ref[0, z, 0].astype(F32)
        refs[z - 4][0, 0] = both.astype(BF)


def sum_z_first(keep, got, start):
    block = pl.BlockSpec((1, 4, 1, 96, D), lambda d, e: (d, 0, start + e, 0, 0))
    here, ahead, across, behind = kernel_call(
        join_rings_kernel,
        "join_rings",
        [shaped(BF, 2, 2, 96, D)] * 4,
        grid=(2, 2),
        in_specs=[block, block],
        out_specs=[pl.BlockSpec((1, 1, 96, D), lambda d, e: (d, e, 0, 0))] * 4,
    )(keep, got)
    came = [send(ahead, "ctx", up), send(behind, "ctx", down), send(across, "ctx", far)]
    half = lambda d: here[d].astype(F32) + sum(v[d].astype(F32) for v in came)
    return half(0) + send(half(1).astype(BF), "dp", beside).astype(F32), came, here


def join_z_kernel(own_ref, got_ref, *refs):
    for z in range(4):
        refs[z - 4][0] = (own_ref[z, 0].astype(F32) + got_ref[z, 0].astype(F32)).astype(BF)


def sum_z(own, got, after):
    block = pl.BlockSpec((4, 1, 96, D), lambda e: (0, e, 0, 0))
    here, ahead, across, behind = kernel_call(
        join_z_kernel,
        "join_z",
        [shaped(BF, 2, 96, D)] * 4,
        grid=(2,),
        in_specs=[block, block] + [ANY] * len(after),
        out_specs=[pl.BlockSpec((1, 96, D), lambda e: (e, 0, 0))] * 4,
    )(own, got, *after)
    came = [send(ahead, "ctx", up), send(behind, "ctx", down), send(across, "ctx", far)]
    return here.astype(F32) + sum(v.astype(F32) for v in came), came, here


def join_kv_kernel(mine_ref, got_ref, *refs):
    own, outs = refs[-4], refs[-3:]
    own[...] = mine_ref[0].astype(F32) + got_ref[0].astype(F32)
    for k in range(3):
        outs[k][...] = (mine_ref[k + 1].astype(F32) + got_ref[k + 1].astype(F32)).astype(BF)


def to_all(value, axis):
    return lax.all_to_all(value, axis, 0, 0, tiled=True)


def local(
    tokens,
    doc_ids,
    gain_attn,
    w_qkv,
    w_out,
    gain_ffn,
    w_router,
    routes,
    w_gate,
    w_up,
    w_down,
    grad_output,
):
    vmem = pl.BlockSpec(memory_space=pltpu.VMEM)
    ctx = lax.axis_index("ctx")
    me = lax.axis_index("expert")
    gain_first = gain_attn.astype(F32)[None, :]
    gain_second = gain_ffn.astype(F32)[None, :]

    named = jnp.pad(routes[0].astype(BF), ((0, 0), (0, TILE - 8)))
    told = jnp.concatenate([grad_output[0], named], axis=1)
    told = lax.all_gather(told, "expert", axis=0)

    places = ctx * ROWS + jnp.arange(ROWS, dtype=jnp.int32)
    lane = jnp.arange(TILE)
    frequency = 10000.0 ** (-(lane % 32).astype(F32) / (HD // 2))
    angles = places.astype(F32)[:, None] * frequency[None, :]
    cosine = jnp.cos(angles)
    sine = jnp.sin(angles) * jnp.where(lane % HD < HD // 2, -1.0, 1.0)[None, :]
    normed, q_pad, kv_own = kernel_call(
        first_kernel,
        "project",
        (shaped(BF, ROWS, D), shaped(BF, 4, 4 * ROWS, TILE), shaped(BF, ROWS, D)),
    )(tokens[0], gain_first, w_qkv, cosine, sine)

    normed_all = lax.all_gather(normed, "expert", axis=0, tiled=True)
    kv_mine = [send(kv_own, "ctx", to) for to in (down, up, far)]
    kv_beside = send(kv_own, "ctx", beside)
    kv_mine = jnp.stack(kv_mine)
    kv_other = send(kv_mine, "ctx", beside)
    keys = (kv_own, kv_beside, kv_mine, kv_other)

    docs = doc_ids[0].reshape(8, ROWS)
    ring = jnp.array([0, 2, -2, 4], jnp.int32)
    block_ids = jnp.concatenate([ctx + ring, jnp.bitwise_xor(ctx, 1) + ring]) % 8
    picks = (block_ids[:, None] == jnp.arange(8)[None, :]).astype(jnp.int32)
    key_docs = jnp.sum(picks[:, :, None] * docs[None], axis=1).reshape(-1)
    key_places = (block_ids[:, None] * ROWS + jnp.arange(ROWS)[None, :]).reshape(-1)
    own_docs = jnp.sum((jnp.arange(8) == ctx).astype(jnp.int32)[:, None] * docs, axis=0)
    row_info = jnp.stack([places, own_docs])
    key_info = jnp.stack([key_places, key_docs]).astype(jnp.int32)

    heads, lse, middle, normed_ffn = kernel_call(
        attend_kernel,
        "attend",
        (
            shaped(BF, ROWS, D),
            shaped(F32, ROWS, TILE),
            shaped(F32, ROWS, D),
            shaped(BF, ROWS, D),
        ),
        scratch_shapes=[pltpu.VMEM((8 * ROWS, D), BF)],
    )(q_pad, *keys, row_info.T, key_info, w_out, tokens[0], gain_second)

    heads_all = lax.all_gather(heads, "expert", axis=0, tiled=True)

    from_up, from_down, from_far = (send(normed_ffn, "expert", to) for to in (down, up, far))
    from_beside = send(normed_ffn, "expert", beside)
    other_up, other_down = (send(from_beside, "expert", to) for to in (down, up))
    other_far = send(from_far, "expert", beside)
    router_rel = jnp.roll(w_router, -4 * me, axis=1).T
    pair = jnp.bitwise_xor(me, 1)
    order = [me, pair, up(me), (me + 6) % 8, far(me), up(pair), (pair + 6) % 8, far(pair), me]
    order += [lax.axis_index("dp"), ctx // 2, ctx % 2]
    blocks = (normed_ffn, from_beside, from_up, from_down)
    blocks += (from_far, other_up, other_down, other_far)
    made, back, keep, give = experts(
        jnp.stack(order).astype(jnp.int32), blocks, told, router_rel, w_gate, w_up, w_down
    )
    back = to_all(back, "expert")
    given = send(give, "ctx", beside)
    own_0, other_0 = join_x(keep, given, 0, [])
    crossed_0 = send(other_0, "dp", beside)
    sums_1, came_1, own_1 = sum_z_first(keep, given, 2)
    made = lax.psum_scatter(made.reshape(8 * ROWS, D), "expert", tiled=True)
    router_wide = jnp.pad(w_router, ((0, 0), (0, TILE - 32)))
    operands = (
        back,
        normed_ffn,
        middle,
        grad_output[0],
        gain_second,
        routes[0],
        router_wide,
        w_out,
    )
    grad_middle, rest, g_pad, branch = kernel_call(
        middle_kernel,
        "middle_back",
        (
            shaped(F32, ROWS, D),
            shaped(F32, D, TILE),
            shaped(BF, 4, 4 * ROWS, TILE),
            shaped(BF, 8, ROWS, TILE),
        ),
        in_specs=[vmem] * len(operands),
    )(*operands)
    cols, grad_q, dkv_mine, dkv_other = kernel_call(
        back_kernel,
        "attend_back",
        (
            shaped(BF, 8, ROWS, 2 * TILE),
            shaped(BF, ROWS, D),
            shaped(BF, 4, ROWS, D),
            shaped(BF, 4, ROWS, D),
        ),
        in_specs=[vmem] * 12 + [ANY] * 3,
        scratch_shapes=[pltpu.VMEM((8 * ROWS, D), BF)],
    )(g_pad, q_pad, *keys, lse, row_info, key_info.T, cosine, sine, branch, *came_1)

    own, *parts = kernel_call(
        join_kv_kernel,
        "join_kv",
        [shaped(F32, ROWS, D)] + [shaped(BF, ROWS, D)] * 3,
        in_specs=[vmem] * 2 + [ANY],
    )(dkv_mine, send(dkv_other, "ctx", beside), crossed_0)
    arrived = [send(v, "ctx", to) for v, to in zip(parts, (up, down, far))]
    sums_0, came_0, here_0 = sum_z(own_0, crossed_0, [own])
    cols = kernel_call(
        turn_kernel, "turn", shaped(BF, 8, ROWS, 3 * TILE), in_specs=[vmem] * 7 + [ANY]
    )(own, *arrived, cosine, sine, cols, here_0)
    here = to_all(cols, "expert")
    here = here.reshape(8 * ROWS, 3 * TILE)
    grad_tokens, side = kernel_call(
        last_kernel,
        "grad_tokens",
        (shaped(BF, ROWS, D), shaped(BF, D, TILE)),
        in_specs=[vmem] * 7 + [ANY] * 3,
    )(grad_q, cols, w_qkv, tokens[0], gain_first, grad_middle, rest, *came_0)
    output = (middle + made.astype(F32)).astype(BF)

    out_cols = mm(heads_all, here[:, :TILE], TN).astype(BF)
    mixed_cols = mm(normed_all, here[:, TILE:], TN).astype(BF)
    dense = jnp.concatenate([mixed_cols, out_cols, side], axis=1)
    dense = jnp.sum(to_all(dense.reshape(16, 64, 4 * TILE), ("dp", "ctx")).astype(F32), axis=0)
    dense = to_all(dense.astype(BF).reshape(8, 8, 4 * TILE), "expert").astype(F32)
    tiles = jnp.transpose(dense[:, :, : 3 * TILE].reshape(8, 8, 3, TILE), (1, 2, 0, 3))
    rest = jnp.sum(dense[:, :, 3 * TILE :], axis=0)
    parts = jnp.concatenate([sums_0, sums_1], axis=0)
    return (
        output[None],
        grad_tokens[None],
        rest[:, 32],
        tiles[:, :2].reshape(8, 2 * D),
        tiles[:, 2].reshape(8, D),
        rest[:, 33],
        rest[:, :32],
        parts[:, :64, :FF],
        parts[:, :64, FF:],
        parts[:, 64:, :],
    )


def solution(mesh):
    in_specs = (
        P(("dp", "expert"), "ctx", None),
        P(("dp", "expert"), None),
        P(),
        P(),
        P(),
        P(),
        P(),
        P(("dp", "expert"), "ctx", None),
        P("expert", None, None),
        P("expert", None, None),
        P("expert", None, None),
        P(("dp", "expert"), "ctx", None),
    )
    out_specs = (
        P(("dp", "expert"), "ctx", None),
        P(("dp", "expert"), "ctx", None),
        P(("dp", "ctx", "expert")),
        P(("dp", "ctx", "expert"), None),
        P(("dp", "ctx", "expert"), None),
        P(("dp", "ctx", "expert")),
        P(("dp", "ctx", "expert"), None),
        P("expert", ("dp", "ctx"), None),
        P("expert", ("dp", "ctx"), None),
        P("expert", ("dp", "ctx"), None),
    )
    return jax.shard_map(local, mesh=mesh, in_specs=in_specs, out_specs=out_specs, check_vma=False)
```
